32 devices in a mesh: group: 2 (over x), seq: 4 (over z), tensor: 4 (over y, core).
Axes of the slice: x: 2, y: 2, z: 4, core: 2. Of those that a mesh axis runs over, the one named last changes fastest.
Arguments:
- tokens: bfloat16 [2, 512, 8192], P('group', 'seq', 'tensor'), may hold values from -6 to 6
- frame_feats: bfloat16 [2, 32, 1280], P('group', 'seq'), may hold values from -6 to 6
- w_proj: bfloat16 [1280, 8192], P(None, 'tensor'), may hold values from -0.15625 to 0.15625
- frame_pos: int32 [2, 32], P('group', 'seq'), may hold values from 0 to 511, as said below
- segments: int32 [2, 512], P('group', 'seq'), may hold values from 0 to 3, never falling along the last dimension, each value on 1 to 256 neighbouring positions
- signs: int32 [2, 512], P('group', 'seq'), may hold values from 0 to 1
- w_x: bfloat16 [8192, 8192], P(('group', 'seq'), 'tensor'), may hold values from -0.0625 to 0.0625
- w_bc: bfloat16 [8192, 2048], P(('group', 'seq'), 'tensor'), may hold values from -0.0625 to 0.0625
- w_dt: bfloat16 [8192, 128], P(('group', 'seq'), 'tensor'), may hold values from -0.0625 to 0.0625
- dt_bias: float32 [128], P('tensor'), may hold values from -4 to -2
- decay_rate: float32 [128], P('tensor'), may hold values from 0.0001 to 1
- skip_gain: float32 [128], P('tensor'), may hold values from 0.5 to 6
- probe: bfloat16 [2, 512, 8192], P('group', 'seq', 'tensor'), may hold values from -6 to 6
Outputs:
- adv_tokens: bfloat16 [2, 512, 8192], P('group', 'seq', 'tensor')
- adv_frames: bfloat16 [2, 32, 8192], P('group', 'seq', 'tensor')
The draws below stay inside these ranges and needn't reach their ends.
Inputs may be any that keep to these rules, and one draw needn't show every extreme that they name: `frame_pos`: within a sample the positions are distinct; frame token k * 8 + b * 2 + i (0 <= i < 2) lies in positions b * 128 to (b + 1) * 128 - 1. `segments`: document ids never fall along a sample.
All inputs are finite; a program needn't handle non-finite values.
Results may differ from the reference program's by a relative error of at most 0.0095.
Values may be sent and summed in bfloat16 or wider, within the bound.
A program may use at most 128 MiB of HBM per device.

```python
import math
import jax
import jax.numpy as jnp
import numpy as np
from jax import lax

D = 8192
HEADS = 128
HEAD_DIM = 64
STATE = 128
GROUPS = 8
DV = 1280
TOK_DEV = 128
FB = 2
SEQ_LEN = 512
F_DEV = 8
FRAMES = 32
SAMPLES = 2
N_TENSOR = 4


def draw_frame_pos(key, part):
    shards = F_DEV // FB
    keys = jax.random.split(jax.random.fold_in(key, 11), SAMPLES * shards)

    def one_shard(shard_key):
        return jax.random.permutation(shard_key, TOK_DEV)[:F_DEV].astype(jnp.int32)
    slots = jax.vmap(one_shard)(keys).reshape(SAMPLES, shards, shards, FB)
    offset = (jnp.arange(shards, dtype=jnp.int32) * TOK_DEV)[None, :, None, None]
    placed = slots + offset
    return jnp.transpose(placed, (0, 2, 1, 3)).reshape(SAMPLES, FRAMES).astype(jnp.int32)


def place_ends(values, rng, low, largest):
    dims = values.shape
    spot = [jax.random.randint(jax.random.fold_in(rng, axis), (), 0, dims[axis]) for axis in range(len(dims))]
    values = values.at[tuple(spot)].set(low)
    longest = dims.index(max(dims))
    spot[longest] = (spot[longest] + 1) % dims[longest]
    return values.at[tuple(spot)].set(largest)


def block_scale(key, shape, pieces, low, high):
    def one(dim, parts):
        steps = jax.random.uniform(jax.random.fold_in(jax.random.fold_in(key, 6), dim), (parts,), jnp.float32, low / len(pieces), high / len(pieces))
        return jnp.repeat(jnp.exp(steps), shape[dim] // parts).reshape((-1,) + (1,) * (len(shape) - dim - 1))

    gain = one(*pieces[0])
    for cut in pieces[1:]:
        gain = gain * one(*cut)
    return gain


def length_profile(count, total, limit, lean):
    weights = [(1 << 20) // math.isqrt(grade ** lean) + 1 for grade in range(2, count + 1)]
    surplus, holding = total - limit - (count - 1), [1] * (count - 1)
    while surplus > 0:
        candidates = [i for i in range(count - 1) if holding[i] < limit]
        mass, budget = sum([weights[i] for i in candidates]), surplus
        for i in candidates:
            extra = min(limit - holding[i], max(1, budget * weights[i] // mass), surplus)
            holding[i] = holding[i] + extra
            surplus = surplus - extra
    return np.array([limit] + holding)


def ragged_sizes(own_key, number_of, total, most, slope):
    if number_of == 2:
        one = jax.random.randint(own_key, (), max(1, total - most), min(most, total - 1) + 1)
        return jnp.stack([one, total - one])
    tallies = jnp.asarray(length_profile(number_of, total, most, slope), jnp.int32)
    couples = (number_of - 1) // 2
    giver, receiver = tallies[1:1 + 2 * couples:2], tallies[2:2 + 2 * couples:2]
    slack = jnp.minimum(giver - 1, most - receiver)
    moved = jax.random.randint(jax.random.fold_in(own_key, 1), (couples,), 0, 1 << 20) % (slack + 1)
    tallies = tallies.at[1:1 + 2 * couples:2].set(giver - moved).at[2:2 + 2 * couples:2].set(receiver + moved)
    return tallies[jax.random.permutation(jax.random.fold_in(own_key, 2), number_of)]


def noise(stream_key, extent, deviation, reach, pieces=(), held_as=jnp.bfloat16):
    loudness = block_scale(stream_key, extent, pieces, -0.22, 0.18) if pieces else 1.0
    values = jax.random.normal(stream_key, extent, jnp.float32) * deviation * loudness
    return jnp.minimum(jnp.maximum(values, -reach), reach).astype(held_as)


def setup_inputs(seed: int = 0) -> dict:
    seeds = jax.random.split(jax.random.key(seed), 14)
    return {
        "tokens": noise(seeds[0], (SAMPLES, SEQ_LEN, D), 1.0, 6.0, ((0, 2), (1, 4), (2, 4))),
        "frame_feats": noise(seeds[1], (SAMPLES, FRAMES, DV), 1.0, 6.0, ((0, 2), (1, 4))),
        "w_proj": noise(seeds[2], (DV, D), DV ** -0.5, 0.15625, ((1, 4),)),
        "frame_pos": draw_frame_pos(jax.random.fold_in(seeds[13], 71), 0),
        "segments": jax.vmap(lambda own: jnp.searchsorted(jnp.cumsum(ragged_sizes(own, 4, SEQ_LEN, SEQ_LEN // 2, 1)), jnp.arange(SEQ_LEN), side="right"))(jax.random.split(seeds[4], SAMPLES)).reshape((SAMPLES, SEQ_LEN)).astype(jnp.int32),
        "signs": place_ends(jax.random.randint(seeds[5], (SAMPLES, SEQ_LEN), 0, 2), jax.random.fold_in(seeds[5], 1), 0, 1).astype(jnp.int32),
        "w_x": noise(seeds[6], (D, HEADS * HEAD_DIM), D ** -0.5, 0.0625, ((0, 8), (1, 4))),
        "w_bc": noise(seeds[7], (D, GROUPS * 2 * STATE), D ** -0.5, 0.0625, ((0, 8), (1, 4))),
        "w_dt": noise(seeds[8], (D, HEADS), D ** -0.5, 0.0625, ((0, 8), (1, 4))),
        "dt_bias": jnp.clip(-4.0 + 2.0 * jax.random.uniform(seeds[9], (HEADS,), jnp.float32) ** block_scale(seeds[9], (HEADS,), ((0, 4),), -0.2, 0.2), -4.0, -2.0),
        "decay_rate": jnp.clip(jnp.exp(math.log(1.0) - 9.2103404 * jax.random.uniform(seeds[10], (HEADS,), jnp.float32) ** block_scale(seeds[10], (HEADS,), ((0, 4),), -0.2, 0.2)), 0.0001, 1.0),
        "skip_gain": jnp.clip(0.5 + 5.5 * jax.random.uniform(seeds[11], (HEADS,), jnp.float32) ** block_scale(seeds[11], (HEADS,), ((0, 4),), -0.2, 0.2), 0.5, 6.0),
        "probe": noise(seeds[12], (SAMPLES, SEQ_LEN, HEADS * HEAD_DIM), 1.0, 6.0, ((0, 2), (1, 4), (2, 4))),
    }


precise = lax.Precision.HIGHEST

def split_proj(proj_x, proj_bc, proj_dt, dt_bias):
    count = proj_x.shape[0]
    values = proj_x.reshape(count, -1, HEAD_DIM)
    pairs = proj_bc.reshape(count, -1, 2, STATE)
    step_sizes = jax.nn.softplus(proj_dt + dt_bias[None, :])
    return (values, pairs[:, :, 0], pairs[:, :, 1], step_sizes)

def block_state(proj_x, proj_bc, proj_dt, dt_bias, decay_rate, segment, seg_prev):
    values, b_proj, c_proj, step_sizes = split_proj(proj_x, proj_bc, proj_dt, dt_bias)
    repeat = values.shape[1] // b_proj.shape[1]
    log_decay = jnp.cumsum(-step_sizes * decay_rate[None, :], axis=0)
    end_decay = log_decay[-1]
    same_end = (segment == segment[-1])[:, None]
    tail_weight = jnp.where(same_end, jnp.exp(end_decay[None, :] - log_decay), 0.0) * step_sizes
    b_heads = jnp.repeat(b_proj, repeat, axis=1)
    end_states = jnp.einsum('sh,shp,shn->hpn', tail_weight, values, b_heads, precision=precise)
    carry_decay = jnp.where(segment[-1] == seg_prev, jnp.exp(end_decay), 0.0)
    return (end_states, carry_decay)

def block_loss(proj_x, proj_bc, proj_dt, dt_bias, decay_rate, skip_gain, segment, seg_prev, carried_in, probe):
    values, b_proj, c_proj, step_sizes = split_proj(proj_x, proj_bc, proj_dt, dt_bias)
    repeat = values.shape[1] // b_proj.shape[1]
    count = values.shape[0]
    log_decay = jnp.cumsum(-step_sizes * decay_rate[None, :], axis=0)
    position = jnp.arange(count)
    visible = (segment[:, None] == segment[None, :]) & (position[:, None] >= position[None, :])
    visible = visible[:, :, None]
    gap_decay = log_decay[:, None, :] - log_decay[None, :, :]
    decay = jnp.where(visible, jnp.exp(jnp.where(visible, gap_decay, 0.0)), 0.0)
    scores = jnp.einsum('tgn,sgn->tsg', c_proj, b_proj, precision=precise)
    scores = jnp.repeat(scores, repeat, axis=2)
    mixed = decay * scores * step_sizes[None, :, :]
    within = jnp.einsum('tsh,shp->thp', mixed, values, precision=precise)
    c_heads = jnp.repeat(c_proj, repeat, axis=1)
    carry_scale = jnp.where((segment == seg_prev)[:, None], jnp.exp(log_decay), 0.0)
    carried = jnp.einsum('thn,hpn->thp', c_heads, carried_in, precision=precise) * carry_scale[:, :, None]
    result = within + carried + skip_gain[None, :, None] * values
    return jnp.sum(result.reshape(count, -1) * probe.astype(jnp.float32))

def sample_step(tokens, frame_feats, w_proj, frame_pos, segments, sign_bits, w_x, w_bc, w_dt, dt_bias, decay_rate, skip_gain, probe):
    frame_emb = jnp.dot(frame_feats, w_proj, preferred_element_type=jnp.float32).astype(jnp.bfloat16)
    merged = tokens.at[frame_pos].set(frame_emb)
    proj_x = jnp.dot(merged, w_x, preferred_element_type=jnp.float32)
    proj_bc = jnp.dot(merged, w_bc, preferred_element_type=jnp.float32)
    proj_dt = jnp.dot(merged, w_dt, preferred_element_type=jnp.float32)
    blocks = SEQ_LEN // TOK_DEV
    seg_blocks = segments.reshape(blocks, TOK_DEV)
    seg_prev = jnp.concatenate([jnp.zeros((1,), jnp.int32), seg_blocks[:-1, -1].astype(jnp.int32)])
    probe_blocks = probe.reshape(blocks, TOK_DEV, -1)

    def total(px, pbc, pdt):
        bx = px.reshape(blocks, TOK_DEV, -1)
        bbc = pbc.reshape(blocks, TOK_DEV, -1)
        bdt = pdt.reshape(blocks, TOK_DEV, -1)

        def state_item(item):
            return block_state(item[0], item[1], item[2], dt_bias, decay_rate, item[3], item[4])
        end_states, decays = lax.map(state_item, (bx, bbc, bdt, seg_blocks, seg_prev))

        def advance(state, item):
            return (item[0][:, None, None] * state + item[1], state)
        _, entering = lax.scan(advance, jnp.zeros(end_states.shape[1:], jnp.float32), (decays, end_states))

        def loss_item(item):
            return block_loss(item[0], item[1], item[2], dt_bias, decay_rate, skip_gain, item[3], item[4], item[5], item[6])
        losses = lax.map(jax.checkpoint(loss_item), (bx, bbc, bdt, seg_blocks, seg_prev, entering, probe_blocks))
        return jnp.sum(losses)
    _, pull = jax.vjp(total, proj_x, proj_bc, proj_dt)
    grad_x, grad_bc, grad_dt = pull(jnp.ones((), jnp.float32))
    grad_x = grad_x.astype(jnp.bfloat16)
    grad_bc = grad_bc.astype(jnp.bfloat16)
    grad_dt = grad_dt.astype(jnp.bfloat16)
    width_x = grad_x.shape[1] // N_TENSOR
    width_bc = grad_bc.shape[1] // N_TENSOR
    width_dt = grad_dt.shape[1] // N_TENSOR
    gradient = jnp.zeros(merged.shape, jnp.float32)
    for j in range(N_TENSOR):
        part = jnp.dot(grad_x[:, j * width_x:(j + 1) * width_x], w_x[:, j * width_x:(j + 1) * width_x].T, preferred_element_type=jnp.float32)
        part = part + jnp.dot(grad_bc[:, j * width_bc:(j + 1) * width_bc], w_bc[:, j * width_bc:(j + 1) * width_bc].T, preferred_element_type=jnp.float32)
        part = part + jnp.dot(grad_dt[:, j * width_dt:(j + 1) * width_dt], w_dt[:, j * width_dt:(j + 1) * width_dt].T, preferred_element_type=jnp.float32)
        gradient = gradient + lax.optimization_barrier(part.astype(jnp.bfloat16)).astype(jnp.float32)
    grad_scale = jnp.sqrt(jnp.mean(gradient * gradient) + 1e-06)
    direction = (2 * sign_bits - 1).astype(jnp.float32)[:, None]
    adv = (merged.astype(jnp.float32) + 0.5 * direction * gradient / grad_scale).astype(jnp.bfloat16)
    return (adv, adv[frame_pos])

def reference(tokens, frame_feats, w_proj, frame_pos, segments, signs, w_x, w_bc, w_dt, dt_bias, decay_rate, skip_gain, probe):
    token_outs = []
    frame_outs = []
    for sample in range(SAMPLES):
        adv, frames = sample_step(tokens[sample], frame_feats[sample], w_proj, frame_pos[sample], segments[sample], signs[sample], w_x, w_bc, w_dt, dt_bias, decay_rate, skip_gain, probe[sample])
        token_outs.append(adv)
        frame_outs.append(frames)
    return (jnp.stack(token_outs), jnp.stack(frame_outs))
```

```python
import jax
import jax.numpy as jnp
from jax import lax
from jax.sharding import PartitionSpec as P

HEAD_DIM = 64
STATE = 128
BF16 = jnp.bfloat16
F32 = jnp.float32


def mixer_grad(x, b, c, pdt, probe, seg, dt_bias, decay_rate, skip_gain):
    count, heads = pdt.shape
    shifted = pdt + dt_bias[None, :]
    dt = jax.nn.softplus(shifted).T
    ld = jnp.cumsum(-dt * decay_rate[:, None], axis=1)
    position = jnp.arange(count)
    visible = (seg[:, None] == seg[None, :]) & (position[:, None] >= position[None, :])
    gap = ld[:, :, None] - ld[:, None, :]
    decay = jnp.where(visible[None], jnp.exp(jnp.where(visible[None], gap, 0.0)), 0.0)
    xh = x.astype(BF16).reshape(count, heads, HEAD_DIM)
    ph = probe.reshape(count, heads, HEAD_DIM)
    bb, cb = b.astype(BF16), c.astype(BF16)
    scores = jnp.dot(cb, bb.T, preferred_element_type=F32)
    pairs = jnp.einsum("thp,shp->hts", ph, xh, preferred_element_type=F32)
    mixed = decay * scores[None]
    grad_x = jnp.einsum("hts,thp->shp", mixed.astype(BF16), ph, preferred_element_type=F32)
    grad_x = grad_x * dt.T[:, :, None] + skip_gain[None, :, None] * ph.astype(F32)
    weighted = mixed * pairs
    col = jnp.sum(weighted, axis=1)
    row = jnp.sum(weighted * dt[:, None, :], axis=2)
    grad_s = jnp.sum(decay * pairs * dt[:, None, :], axis=0).astype(BF16)
    grad_c = jnp.dot(grad_s, bb, preferred_element_type=F32)
    grad_b = jnp.dot(grad_s.T, cb, preferred_element_type=F32)
    grad_ld = row - col * dt
    later = jnp.cumsum(grad_ld[:, ::-1], axis=1)[:, ::-1]
    grad_dt = (col - decay_rate[:, None] * later).T * jax.nn.sigmoid(shifted)
    return grad_x.reshape(count, -1), grad_b, grad_c, grad_dt


def body(
    tokens,
    frame_feats,
    w_proj,
    frame_pos,
    segments,
    signs,
    w_x,
    w_bc,
    w_dt,
    dt_bias,
    decay_rate,
    skip_gain,
    probe,
):
    rows = tokens.shape[1]
    groups, shards, tensors = (lax.axis_size(a) for a in ("group", "seq", "tensor"))
    g, s, t = (lax.axis_index(a) for a in ("group", "seq", "tensor"))
    parts = groups * shards
    count = rows * shards
    width = w_x.shape[0]
    heads = w_dt.shape[1] // shards
    per_group = w_dt.shape[1] * 2 * STATE // w_bc.shape[1]
    cols_x = heads * HEAD_DIM
    group_of = [(k * heads) // per_group for k in range(shards)]
    cols = cols_x + 2 * STATE + heads

    feats, pos = (
        lax.all_to_all(frame_feats[0], "seq", split_axis=0, concat_axis=0, tiled=True),
        lax.all_to_all(frame_pos[0], "seq", split_axis=0, concat_axis=0, tiled=True),
    )
    local_pos = pos - s * rows
    arrived = jnp.dot(feats, w_proj, preferred_element_type=F32).astype(BF16)
    merged = tokens[0].at[local_pos].set(arrived)

    sub = rows // tensors
    f = lax.all_to_all(merged, "tensor", split_axis=0, concat_axis=1, tiled=True)
    f = f.reshape(sub, parts, width).transpose(1, 0, 2)
    f = lax.all_to_all(f, ("group", "seq"), split_axis=0, concat_axis=0, tiled=True)
    f = lax.all_gather(f, "tensor", axis=1, tiled=True)
    f = f.reshape(groups, count, width)

    weights = jnp.stack(
        [
            jnp.concatenate(
                [
                    w_x[:, k * cols_x : (k + 1) * cols_x],
                    w_bc[:, group_of[k] * 2 * STATE : (group_of[k] + 1) * 2 * STATE],
                    w_dt[:, k * heads : (k + 1) * heads],
                ],
                axis=1,
            )
            for k in range(shards)
        ]
    )
    partial = jnp.einsum("gtk,skc->gstc", f, weights, preferred_element_type=F32).astype(BF16)
    proj = lax.psum_scatter(
        partial.reshape(parts, count, cols), ("group", "seq"), scatter_dimension=0, tiled=False
    ).astype(F32)

    seg = lax.all_gather(segments[0], "seq", axis=0, tiled=True)
    prb = lax.all_to_all(
        probe[0].reshape(rows, shards, cols_x).transpose(1, 0, 2),
        "seq",
        split_axis=0,
        concat_axis=0,
        tiled=True,
    ).reshape(count, cols_x)

    def own(v):
        return lax.dynamic_slice(v, (s * heads,), (heads,))

    grads = mixer_grad(
        proj[:, :cols_x],
        proj[:, cols_x : cols_x + STATE],
        proj[:, cols_x + STATE : cols_x + 2 * STATE],
        proj[:, cols_x + 2 * STATE :],
        prb,
        seg,
        own(dt_bias),
        own(decay_rate),
        own(skip_gain),
    )
    grads = jnp.concatenate([v.astype(BF16) for v in grads], axis=1)
    every = lax.all_gather(grads, ("group", "seq"), axis=0, tiled=False)
    every = every.reshape(groups, shards, count, cols)
    back = jnp.einsum("gstc,skc->gtk", every, weights, preferred_element_type=F32).astype(BF16)

    back = back.reshape(parts, tensors, sub, width).transpose(1, 0, 2, 3)
    back = lax.all_to_all(back, "tensor", split_axis=0, concat_axis=0, tiled=True)
    summed = jnp.sum(back.astype(F32), axis=0)
    squares = jnp.sum(summed.reshape(groups, -1) ** 2, axis=1)
    squares = lax.psum(squares, ("group", "seq", "tensor"))[g]
    home = lax.all_to_all(
        summed.astype(BF16), ("group", "seq"), split_axis=0, concat_axis=0, tiled=True
    )
    home = home.transpose(1, 0, 2).reshape(sub, tensors, -1).transpose(1, 0, 2)
    gradient = lax.all_to_all(home, "tensor", split_axis=0, concat_axis=0, tiled=True)
    gradient = gradient.reshape(rows, -1).astype(F32)

    entries = count * parts * width
    grad_scale = jnp.sqrt(squares / entries + 1e-06)
    direction = (2 * signs[0] - 1).astype(F32)[:, None]
    adv = (merged.astype(F32) + 0.5 * direction * gradient / grad_scale).astype(BF16)
    picked = adv[local_pos]
    returned = lax.all_to_all(picked, "seq", split_axis=0, concat_axis=0, tiled=True)
    return (adv[None], returned[None])


def solution(mesh):
    return jax.shard_map(
        body,
        mesh=mesh,
        in_specs=(
            P("group", "seq", "tensor"),
            P("group", "seq", None),
            P(None, "tensor"),
            P("group", "seq"),
            P("group", "seq"),
            P("group", "seq"),
            P(("group", "seq"), "tensor"),
            P(("group", "seq"), "tensor"),
            P(("group", "seq"), "tensor"),
            P("tensor"),
            P("tensor"),
            P("tensor"),
            P("group", "seq", "tensor"),
        ),
        out_specs=(P("group", "seq", "tensor"), P("group", "seq", "tensor")),
        check_vma=False,
    )
```

```python
import functools

import jax
import jax.numpy as jnp
from jax import lax
from jax.experimental import pallas as pl
from jax.experimental.pallas import tpu as pltpu
from jax.sharding import PartitionSpec as P

HEAD_DIM = 64
STATE = 128
BF16 = jnp.bfloat16
F32 = jnp.float32


MESH = pl.DeviceIdType.MESH
VMEM_BYTES = 58 * 2**20


def place():
    return tuple(lax.axis_index(a) for a in ("group", "seq", "tensor"))


def rcopy(src, dst, send, recv, device):
    return pltpu.make_async_remote_copy(
        src_ref=src, dst_ref=dst, send_sem=send, recv_sem=recv, device_id=device, device_id_type=MESH
    )


def far_first(i, s, shards):
    down = jnp.where(i < shards - 1 - s, shards - 1 - i, shards - 2 - i)
    up = jnp.where(i < s, i, i + 1)
    other = jnp.where(2 * s < shards, down, up)
    return jnp.where(i == shards - 1, s, other)


def greet(parts, shards, tensors):
    g, s, t = place()
    me = g * shards + s
    barrier = pltpu.get_barrier_semaphore()
    for i in range(1, parts):
        p = lax.rem(me + i, parts)
        pl.semaphore_signal(
            barrier, inc=1, device_id=(p // shards, lax.rem(p, shards), t), device_id_type=MESH
        )
    for m in range(1, tensors):
        pl.semaphore_signal(barrier, inc=1, device_id=(g, s, t ^ m), device_id_type=MESH)
    pl.semaphore_wait(barrier, parts + tensors - 2)


def bits(tensors):
    m, out = 1, []
    while m < tensors:
        out.append(m)
        m *= 2
    return out


def forward_kernel(
    shards, tensors, heads, merged, wcat, wdt, proj, dts,
    turned, feats, outgo, cross, own, line, dt_part, dt_all,
    a_s, a_r, f_s, f_r, h_s, h_r, x_s, x_r, z_s, z_r, d_s, d_r,
):
    parts = 2 * shards
    g, s, t = place()
    me = g * shards + s
    width = feats.shape[-1]
    sub = feats.shape[2]
    per = merged.shape[-1] // width
    count = shards * tensors * sub
    nq = proj.shape[0]
    span = shards // nq

    def peer(i):
        p = lax.rem(me + i, parts)
        return p, (p // shards, lax.rem(p, shards), t)

    greet(parts, shards, tensors)

    def turn(m):
        return rcopy(merged.at[t ^ m], turned.at[t], a_s.at[m], a_r.at[m], (g, s, t ^ m))

    for m in range(1, tensors):
        turn(m).start()
    turned[t] = merged[t]
    for m in range(1, tensors):
        rcopy(
            merged.at[t ^ m], turned.at[t ^ m], a_s.at[m], a_r.at[m], (g, s, t ^ m)
        ).wait_recv()

    def columns(r):
        return (r // per, slice(None), pl.ds(pl.multiple_of(lax.rem(r, per) * width, width), width))

    def spread(i):
        p, device = peer(i)
        return rcopy(turned.at[columns(p)], feats.at[me, t], f_s.at[i], f_r.at[i], device)

    for i in range(1, parts):
        spread(i).start()
    feats[me, t] = turned[columns(me)]
    for i in range(1, parts):
        q = lax.rem(me + parts - i, parts)
        p, device = peer(i)
        rcopy(feats.at[q, t], feats.at[q, t], f_s.at[i], f_r.at[i], device).wait_recv()

    held = [0]
    for m in reversed(bits(tensors)):
        for c in held:
            rcopy(
                feats.at[:, t ^ c], feats.at[:, t ^ c], h_s.at[m | c], h_r.at[m | c], (g, s, t ^ m)
            ).start()
        for c in held:
            rcopy(
                feats.at[:, t ^ c], feats.at[:, t ^ (m | c)], h_s.at[m | c], h_r.at[m | c],
                (g, s, t ^ m),
            ).wait_recv()
        held = held + [m | c for c in held]

    def product(gg, d, q):
        rows = feats[pl.ds(gg * shards + q * span, span)].reshape(count // nq, width)
        return jnp.dot(rows, wcat[d], preferred_element_type=F32)

    def to_cross(d, q):
        return rcopy(outgo.at[d, q], cross.at[d, q], x_s.at[d, q], x_r.at[d, q], (1 - g, s, t))

    def first(i, carry):
        d = far_first(i, s, shards)
        for q in range(nq):
            outgo[d, q] = product(1 - g, d, q).astype(BF16)
            to_cross(d, q).start()
        return carry

    lax.fori_loop(0, shards, first, 0)

    for gg in range(2):
        rows = feats[gg * shards : (gg + 1) * shards].reshape(count, width)
        steps = lax.dot_general(
            wdt[...], rows, (((1,), (1,)), ((), ())), preferred_element_type=F32
        )
        for k in range(shards):
            dt_part[gg * shards + k] = steps[k * heads : (k + 1) * heads]

    def send_dt(i):
        p, device = peer(i)
        return rcopy(dt_part.at[p], dt_all.at[me], d_s.at[i], d_r.at[i], device)

    for i in range(1, parts):
        send_dt(i).start()
    dt_all[me] = dt_part[me]

    def right(d, q):
        return rcopy(own.at[d, q], line.at[d, q], z_s.at[d, q], z_r.at[d, q], (g, s + 1, t))

    def left(d, q):
        slot = jnp.where(d == s - 1, shards, d)
        return rcopy(own.at[d, q], line.at[slot, q], z_s.at[d, q], z_r.at[slot, q], (g, s - 1, t))

    def come(slot, q):
        rcopy(
            line.at[slot, q], line.at[slot, q], z_s.at[slot, q], z_r.at[slot, q], (1 - g, s, t)
        ).wait_recv()

    def second(i, carry):
        d = far_first(i, s, shards)
        for q in range(nq):
            own[d, q] = product(g, d, q).astype(BF16)
        for q in range(nq):
            to_cross(d, q).wait_recv()
            has_more = ((d > s) & (s > 0)) | ((d < s) & (s < shards - 1))

            @pl.when(has_more)
            def _():
                come(d, q)
                own[d, q] = (
                    own[d, q].astype(F32) + cross[d, q].astype(F32) + line[d, q].astype(F32)
                ).astype(BF16)

            @pl.when(jnp.logical_not(has_more))
            def _():
                own[d, q] = (own[d, q].astype(F32) + cross[d, q].astype(F32)).astype(BF16)

            @pl.when(d > s)
            def _():
                right(d, q).start()

            @pl.when(d < s)
            def _():
                left(d, q).start()

        return carry

    lax.fori_loop(0, shards - 1, second, 0)
    for q in range(nq):
        own[s, q] = product(g, s, q).astype(BF16)
    for q in range(nq):
        to_cross(s, q).wait_recv()
        own[s, q] = (own[s, q].astype(F32) + cross[s, q].astype(F32)).astype(BF16)

        @pl.when(s > 0)
        def _():
            come(s, q)
            own[s, q] = (own[s, q].astype(F32) + line[s, q].astype(F32)).astype(BF16)

        @pl.when(s < shards - 1)
        def _():
            come(shards, q)
            own[s, q] = (own[s, q].astype(F32) + line[shards, q].astype(F32)).astype(BF16)

        proj[q] = own[s, q]

    for i in range(1, parts):
        q = lax.rem(me + parts - i, parts)
        p, device = peer(i)
        rcopy(dt_part.at[p], dt_all.at[q], d_s.at[i], d_r.at[i], device).wait_recv()
    total = dt_all[0]
    for p in range(1, parts):
        total = total + dt_all[p]
    dts[...] = total

    for m in range(1, tensors):
        turn(m).wait_send()
    for i in range(1, parts):
        spread(i).wait_send()
        send_dt(i).wait_send()
    held = [0]
    for m in reversed(bits(tensors)):
        for c in held:
            rcopy(
                feats.at[:, t ^ c], feats.at[:, t ^ c], h_s.at[m | c], h_r.at[m | c], (g, s, t ^ m)
            ).wait_send()
        held = held + [m | c for c in held]

    def last(d, carry):
        for q in range(nq):
            to_cross(d, q).wait_send()

            @pl.when(d > s)
            def _():
                right(d, q).wait_send()

            @pl.when(d < s)
            def _():
                left(d, q).wait_send()

        return carry

    lax.fori_loop(0, shards, last, 0)


def forward(merged, wcat, wdt, shards, tensors, heads):
    parts = 2 * shards
    rows, held = merged.shape
    sub = rows // tensors
    width, cols = wcat.shape[1:]
    count = rows * shards
    nq = 2
    block = (count // nq, cols)
    dma = pltpu.SemaphoreType.DMA
    proj, dts = pl.pallas_call(
        functools.partial(forward_kernel, shards, tensors, heads),
        out_shape=(
            jax.ShapeDtypeStruct((nq,) + block, BF16),
            jax.ShapeDtypeStruct((heads, count), F32),
        ),
        in_specs=[pl.BlockSpec(memory_space=pltpu.VMEM)] * 3,
        out_specs=[pl.BlockSpec(memory_space=pltpu.VMEM)] * 2,
        scratch_shapes=[
            pltpu.VMEM((tensors, sub, held), BF16),
            pltpu.VMEM((parts, tensors, sub, width), BF16),
            pltpu.VMEM((shards, nq) + block, BF16),
            pltpu.VMEM((shards, nq) + block, BF16),
            pltpu.VMEM((shards, nq) + block, BF16),
            pltpu.VMEM((shards + 1, nq) + block, BF16),
            pltpu.VMEM((parts, heads, count), F32),
            pltpu.VMEM((parts, heads, count), F32),
            dma((tensors,)), dma((tensors,)),
            dma((parts,)), dma((parts,)),
            dma((tensors,)), dma((tensors,)),
            dma((shards, nq)), dma((shards, nq)),
            dma((shards + 1, nq)), dma((shards + 1, nq)),
            dma((parts,)), dma((parts,)),
        ],
        compiler_params=pltpu.CompilerParams(
            collective_id=0, has_side_effects=True, vmem_limit_bytes=VMEM_BYTES
        ),
        name="features_project_scatter",
    )(merged.reshape(tensors, sub, held), wcat, wdt)
    return proj.reshape(count, cols), dts


def backward_kernel(
    shards, tensors, merged, grads, gdt, wcat, wdt, step, adv,
    every, dt_all, acc, back, halves, home, mine, tile, tiles_t, tiles_s,
    x_s, x_r, z_s, z_r, d_s, d_r, r_s, r_r, h_s, h_r, m_s, m_r, p_s, p_r, q_s, q_r,
):
    parts = 2 * shards
    g, s, t = place()
    me = g * shards + s
    width = acc.shape[-1]
    sub = merged.shape[1]
    per = merged.shape[-1] // width
    count = shards * tensors * sub
    nq = grads.shape[0]
    span = shards // nq
    deep = tensors * sub

    def peer(i):
        p = lax.rem(me + i, parts)
        return p, (p // shards, lax.rem(p, shards), t)

    greet(parts, shards, tensors)

    def send_dt(i):
        p, device = peer(i)
        return rcopy(gdt, dt_all.at[me], d_s.at[i], d_r.at[i], device)

    def cross(j, q):
        return rcopy(every.at[g, j, q], every.at[g, j, q], x_s.at[j, q], x_r.at[j, q], (1 - g, s, t))

    def right(j, q):
        return rcopy(every.at[g, j, q], every.at[g, j, q], z_s.at[0, j, q], z_r.at[j, q], (g, s + 1, t))

    def left(j, q):
        return rcopy(every.at[g, j, q], every.at[g, j, q], z_s.at[1, j, q], z_r.at[j, q], (g, s - 1, t))

    def each_way(j, q, what):
        @pl.when((j <= s) & (s < shards - 1))
        def _():
            what(right(j, q))

        @pl.when((j >= s) & (s > 0))
        def _():
            what(left(j, q))

        what(cross(j, q))

    for q in range(nq):
        every[g, s, q] = grads[q]
        each_way(s, q, lambda c: c.start())
    for i in range(1, parts):
        send_dt(i).start()
    dt_all[me] = gdt[...]
    for i in range(1, parts):
        q = lax.rem(me + parts - i, parts)
        p, device = peer(i)
        rcopy(gdt, dt_all.at[q], d_s.at[i], d_r.at[i], device).wait_recv()
    for gg in range(2):
        stack = jnp.concatenate([dt_all[gg * shards + k] for k in range(shards)], axis=0)
        acc[gg] = jnp.dot(
            stack.T.astype(BF16), wdt[...], preferred_element_type=F32
        ).reshape(nq, count // nq, width)

    def add(gg, j, q):
        acc[gg, q] += lax.dot_general(
            every[gg, j, q], wcat[j], (((1,), (1,)), ((), ())), preferred_element_type=F32
        )

    def add_cross(j, q):
        rcopy(
            every.at[1 - g, j, q], every.at[1 - g, j, q], x_s.at[j, q], x_r.at[j, q], (1 - g, s, t)
        ).wait_recv()
        add(1 - g, j, q)

    for q in range(nq):
        add(g, s, q)

    def lap(i, carry):
        j = far_first(shards - 1 - i, s, shards)
        before = far_first(shards - i, s, shards)
        for q in range(nq):
            rcopy(
                every.at[g, j, q], every.at[g, j, q], x_s.at[j, q], z_r.at[j, q], (1 - g, s, t)
            ).wait_recv()
            each_way(j, q, lambda c: c.start())
            add(g, j, q)
            add_cross(before, q)
        return carry

    lax.fori_loop(1, shards, lap, 0)

    steps = bits(tensors)

    def reduce_tensor(gg):
        for c in range(shards):
            q, k = c // span, c % span
            back[gg, c] = (
                acc[gg, q, k * deep : (k + 1) * deep].astype(BF16).reshape(tensors, sub, width)
            )
        low, size = 0, tensors
        for n, m in enumerate(steps):
            size //= 2
            bit = lax.rem(t // m, 2)
            keep, give = low + bit * size, low + (1 - bit) * size
            at = tensors - 2 * size
            copy = rcopy(
                back.at[gg, :, pl.ds(give, size)], halves.at[gg, :, pl.ds(at, size)],
                r_s.at[gg, n], r_r.at[gg, n], (g, s, t ^ m),
            )
            copy.start()
            copy.wait_recv()
            back[gg, :, pl.ds(keep, size)] = (
                back[gg, :, pl.ds(keep, size)].astype(F32)
                + halves[gg, :, at : at + size].astype(F32)
            ).astype(BF16)
            copy.wait_send()
            low = keep
        return low

    def send_home(gg, k):
        return rcopy(
            back.at[gg, k, spot], home.at[me], h_s.at[gg * shards + k], h_r.at[me], (gg, k, t)
        )

    spot = reduce_tensor(g)
    for k in range(shards):
        @pl.when(k != s)
        def _():
            send_home(g, k).start()

    home[me] = back[g, s, spot]
    last = far_first(0, s, shards)
    for q in range(nq):
        add_cross(last, q)
    spot = reduce_tensor(1 - g)
    for k in range(shards):
        send_home(1 - g, k).start()
    for i in range(1, parts):
        p, device = peer(i)
        rcopy(home.at[p], home.at[p], h_s.at[p], h_r.at[p], device).wait_recv()

    def turn(m):
        at = pl.ds((t ^ m) * per, per)
        return rcopy(home.at[at], mine.at[spot], m_s.at[m], m_r.at[m], (g, s, t ^ m))

    def spot_of(tt):
        low, size = 0, tensors
        for m in steps:
            size //= 2
            low = low + lax.rem(tt // m, 2) * size
        return low

    for m in range(1, tensors):
        turn(m).start()
    mine[spot] = home[pl.ds(t * per, per)]
    for m in range(1, tensors):
        at = spot_of(t ^ m)
        rcopy(mine.at[at], mine.at[at], m_s.at[m], m_r.at[m], (g, s, t ^ m)).wait_recv()

    total = jnp.zeros((8, 128), F32)
    for n in range(tensors):
        for h in range(per):
            sq = mine[n, h].astype(F32)
            sq = jnp.sum((sq * sq).reshape(sub // 8, 8, width), axis=0)
            for b in range(width // 128):
                total = total + sq[:, b * 128 : (b + 1) * 128]
    tile[0] = total

    def share_t(m):
        return rcopy(tile.at[0], tiles_t.at[m], p_s.at[m], p_r.at[m], (g, s, t ^ m))

    for m in range(1, tensors):
        share_t(m).start()
    for m in range(1, tensors):
        share_t(m).wait_recv()
        total = total + tiles_t[m]
    tile[1] = total

    def share_s(i):
        return rcopy(
            tile.at[1], tiles_s.at[i], q_s.at[i], q_r.at[i], (g, lax.rem(s + i, shards), t)
        )

    for i in range(1, shards):
        share_s(i).start()
    for i in range(1, shards):
        share_s(i).wait_recv()
        total = total + tiles_s[i]
    entries = count * parts * width
    scale = lax.rsqrt(jnp.sum(total, keepdims=True) / entries + 1e-06)
    for n in range(tensors):
        move = step[n] * scale
        for h in range(per):
            at = slice(h * width, (h + 1) * width)
            adv[n, :, at] = (
                merged[n, :, at].astype(F32) + move * mine[n, h].astype(F32)
            ).astype(BF16)

    for i in range(1, parts):
        send_dt(i).wait_send()
    for m in range(1, tensors):
        turn(m).wait_send()
        share_t(m).wait_send()
    for i in range(1, shards):
        share_s(i).wait_send()
    for k in range(shards):
        @pl.when(k != s)
        def _():
            send_home(g, k).wait_send()

        send_home(1 - g, k).wait_send()

    def end(j, carry):
        for q in range(nq):
            each_way(j, q, lambda c: c.wait_send())
        return carry

    lax.fori_loop(0, shards, end, 0)


def backward(merged, grads, gdt, wcat, wdt, direction, shards, tensors):
    parts = 2 * shards
    rows, held = merged.shape
    sub = rows // tensors
    width, cols = wcat.shape[1:]
    count = rows * shards
    per = held // width
    heads = gdt.shape[0]
    nq = 2
    block = (count // nq, cols)
    dma = pltpu.SemaphoreType.DMA
    levels = len(bits(tensors))
    adv = pl.pallas_call(
        functools.partial(backward_kernel, shards, tensors),
        out_shape=jax.ShapeDtypeStruct((tensors, sub, held), BF16),
        in_specs=[pl.BlockSpec(memory_space=pltpu.VMEM)] * 6,
        out_specs=pl.BlockSpec(memory_space=pltpu.VMEM),
        scratch_shapes=[
            pltpu.VMEM((2, shards, nq) + block, BF16),
            pltpu.VMEM((parts, heads, count), F32),
            pltpu.VMEM((2, nq, count // nq, width), F32),
            pltpu.VMEM((2, shards, tensors, sub, width), BF16),
            pltpu.VMEM((2, shards, tensors, sub, width), BF16),
            pltpu.VMEM((parts, sub, width), BF16),
            pltpu.VMEM((tensors, per, sub, width), BF16),
            pltpu.VMEM((2, 8, 128), F32),
            pltpu.VMEM((tensors, 8, 128), F32),
            pltpu.VMEM((shards, 8, 128), F32),
            dma((shards, nq)), dma((shards, nq)),
            dma((2, shards, nq)), dma((shards, nq)),
            dma((parts,)), dma((parts,)),
            dma((2, levels)), dma((2, levels)),
            dma((parts,)), dma((parts,)),
            dma((tensors,)), dma((tensors,)),
            dma((tensors,)), dma((tensors,)),
            dma((shards,)), dma((shards,)),
        ],
        compiler_params=pltpu.CompilerParams(
            collective_id=1, has_side_effects=True, vmem_limit_bytes=VMEM_BYTES
        ),
        name="gather_project_step",
    )(
        merged.reshape(tensors, sub, held),
        grads.reshape((nq,) + block),
        gdt,
        wcat,
        wdt,
        direction.reshape(tensors, sub, 1),
    )
    return adv.reshape(rows, held)


def in_vmem(groups, shards, tensors, rows, width, cols):
    if groups != 2 or shards % 2 or tensors & (tensors - 1) or rows % (16 * tensors):
        return False
    if width % 128 or cols % 128 or shards * width * 2 % tensors:
        return False
    count = rows * shards
    lines = 2 * count * cols * (4 * shards + 1)
    sums = 2 * count * width * 4 + 4 * count * cols * shards
    return max(lines, sums) + 2 * width * cols * shards + 8 * count * width < VMEM_BYTES // 2


def mixer_grad(x, b, c, pdt, probe, seg, dt_bias, decay_rate, skip_gain):
    count, heads = pdt.shape
    shifted = pdt + dt_bias[None, :]
    dt = jax.nn.softplus(shifted).T
    ld = jnp.cumsum(-dt * decay_rate[:, None], axis=1)
    position = jnp.arange(count)
    visible = (seg[:, None] == seg[None, :]) & (position[:, None] >= position[None, :])
    gap = ld[:, :, None] - ld[:, None, :]
    decay = jnp.where(visible[None], jnp.exp(jnp.where(visible[None], gap, 0.0)), 0.0)
    xh = x.astype(BF16).reshape(count, heads, HEAD_DIM)
    ph = probe.reshape(count, heads, HEAD_DIM)
    bb, cb = b.astype(BF16), c.astype(BF16)
    scores = jnp.dot(cb, bb.T, preferred_element_type=F32)
    pairs = jnp.einsum("thp,shp->hts", ph, xh, preferred_element_type=F32)
    mixed = decay * scores[None]
    grad_x = jnp.einsum("hts,thp->shp", mixed.astype(BF16), ph, preferred_element_type=F32)
    grad_x = grad_x * dt.T[:, :, None] + skip_gain[None, :, None] * ph.astype(F32)
    weighted = mixed * pairs
    col = jnp.sum(weighted, axis=1)
    row = jnp.sum(weighted * dt[:, None, :], axis=2)
    grad_s = jnp.sum(decay * pairs * dt[:, None, :], axis=0).astype(BF16)
    grad_c = jnp.dot(grad_s, bb, preferred_element_type=F32)
    grad_b = jnp.dot(grad_s.T, cb, preferred_element_type=F32)
    grad_ld = row - col * dt
    later = jnp.cumsum(grad_ld[:, ::-1], axis=1)[:, ::-1]
    grad_dt = (col - decay_rate[:, None] * later).T * jax.nn.sigmoid(shifted)
    return grad_x.reshape(count, -1), grad_b, grad_c, grad_dt


def body(
    tokens,
    frame_feats,
    w_proj,
    frame_pos,
    segments,
    signs,
    w_x,
    w_bc,
    w_dt,
    dt_bias,
    decay_rate,
    skip_gain,
    probe,
):
    rows = tokens.shape[1]
    groups, shards, tensors = (lax.axis_size(a) for a in ("group", "seq", "tensor"))
    g, s, t = (lax.axis_index(a) for a in ("group", "seq", "tensor"))
    parts = groups * shards
    count = rows * shards
    width = w_x.shape[0]
    heads = w_dt.shape[1] // shards
    per_group = w_dt.shape[1] * 2 * STATE // w_bc.shape[1]
    cols_x = heads * HEAD_DIM
    group_of = [(k * heads) // per_group for k in range(shards)]
    cols = cols_x + 2 * STATE + heads
    sub = rows // tensors

    feats, pos = (
        lax.all_to_all(frame_feats[0], "seq", split_axis=0, concat_axis=0, tiled=True),
        lax.all_to_all(frame_pos[0], "seq", split_axis=0, concat_axis=0, tiled=True),
    )
    local_pos = pos - s * rows
    arrived = jnp.dot(feats, w_proj, preferred_element_type=F32).astype(BF16)
    merged = tokens[0].at[local_pos].set(arrived)

    direct = in_vmem(groups, shards, tensors, rows, width, cols_x + 2 * STATE)
    weights = jnp.stack(
        [
            jnp.concatenate(
                [
                    w_x[:, k * cols_x : (k + 1) * cols_x],
                    w_bc[:, group_of[k] * 2 * STATE : (group_of[k] + 1) * 2 * STATE],
                ]
                + ([] if direct else [w_dt[:, k * heads : (k + 1) * heads]]),
                axis=1,
            )
            for k in range(shards)
        ]
    )
    if direct:
        w_step = w_dt.T
        proj, proj_dt = forward(merged, weights, w_step, shards, tensors, heads)
        proj, proj_dt = proj.astype(F32), proj_dt.T
    else:
        f = lax.all_to_all(merged, "tensor", split_axis=0, concat_axis=1, tiled=True)
        f = f.reshape(sub, parts, width).transpose(1, 0, 2)
        f = lax.all_to_all(f, ("group", "seq"), split_axis=0, concat_axis=0, tiled=True)
        f = lax.all_gather(f, "tensor", axis=1, tiled=True)
        f = f.reshape(groups, count, width)

        partial = jnp.einsum("gtk,skc->gstc", f, weights, preferred_element_type=F32).astype(BF16)
        proj = lax.psum_scatter(
            partial.reshape(parts, count, cols), ("group", "seq"), scatter_dimension=0, tiled=False
        ).astype(F32)
        proj_dt = proj[:, cols_x + 2 * STATE :]

    seg = lax.all_gather(segments[0], "seq", axis=0, tiled=True)
    prb = lax.all_to_all(
        probe[0].reshape(rows, shards, cols_x).transpose(1, 0, 2),
        "seq",
        split_axis=0,
        concat_axis=0,
        tiled=True,
    ).reshape(count, cols_x)

    def own(v):
        return lax.dynamic_slice(v, (s * heads,), (heads,))

    grads = mixer_grad(
        proj[:, :cols_x],
        proj[:, cols_x : cols_x + STATE],
        proj[:, cols_x + STATE : cols_x + 2 * STATE],
        proj_dt,
        prb,
        seg,
        own(dt_bias),
        own(decay_rate),
        own(skip_gain),
    )
    direction = (2 * signs[0] - 1).astype(F32)[:, None]
    if direct:
        wide = jnp.concatenate([v.astype(BF16) for v in grads[:3]], axis=1)
        adv = backward(
            merged, wide, grads[3].T, weights, w_step, 0.5 * direction, shards, tensors
        )
    else:
        grads = jnp.concatenate([v.astype(BF16) for v in grads], axis=1)
        every = lax.all_gather(grads, ("group", "seq"), axis=0, tiled=False)
        every = every.reshape(groups, shards, count, cols)
        back = jnp.einsum("gstc,skc->gtk", every, weights, preferred_element_type=F32).astype(BF16)

        back = back.reshape(parts, tensors, sub, width).transpose(1, 0, 2, 3)
        back = lax.all_to_all(back, "tensor", split_axis=0, concat_axis=0, tiled=True)
        summed = jnp.sum(back.astype(F32), axis=0)
        squares = jnp.sum(summed.reshape(groups, -1) ** 2, axis=1)
        squares = lax.psum(squares, ("group", "seq", "tensor"))[g]
        home = lax.all_to_all(
            summed.astype(BF16), ("group", "seq"), split_axis=0, concat_axis=0, tiled=True
        )
        home = home.transpose(1, 0, 2).reshape(sub, tensors, -1).transpose(1, 0, 2)
        gradient = lax.all_to_all(home, "tensor", split_axis=0, concat_axis=0, tiled=True)
        gradient = gradient.reshape(rows, -1).astype(F32)

        entries = count * parts * width
        grad_scale = jnp.sqrt(squares / entries + 1e-06)
        adv = (merged.astype(F32) + 0.5 * direction * gradient / grad_scale).astype(BF16)
    picked = adv[local_pos]
    returned = lax.all_to_all(picked, "seq", split_axis=0, concat_axis=0, tiled=True)
    return (adv[None], returned[None])


def solution(mesh):
    return jax.shard_map(
        body,
        mesh=mesh,
        in_specs=(
            P("group", "seq", "tensor"),
            P("group", "seq", None),
            P(None, "tensor"),
            P("group", "seq"),
            P("group", "seq"),
            P("group", "seq"),
            P(("group", "seq"), "tensor"),
            P(("group", "seq"), "tensor"),
            P(("group", "seq"), "tensor"),
            P("tensor"),
            P("tensor"),
            P("tensor"),
            P("group", "seq", "tensor"),
        ),
        out_specs=(P("group", "seq", "tensor"), P("group", "seq", "tensor")),
        check_vma=False,
    )
```

```python
import functools

import jax
import jax.numpy as jnp
from jax import lax
from jax.experimental import pallas as pl
from jax.experimental.pallas import tpu as pltpu
from jax.sharding import PartitionSpec as P

HEAD_DIM = 64
STATE = 128
BF16 = jnp.bfloat16
F32 = jnp.float32


MESH = pl.DeviceIdType.MESH
VMEM_BYTES = 58 * 2**20


def place():
    return tuple(lax.axis_index(a) for a in ("group", "seq", "tensor"))


def rcopy(src, dst, send, recv, device):
    return pltpu.make_async_remote_copy(
        src_ref=src, dst_ref=dst, send_sem=send, recv_sem=recv, device_id=device, device_id_type=MESH
    )


def far_first(i, s, shards):
    down = jnp.where(i < shards - 1 - s, shards - 1 - i, shards - 2 - i)
    up = jnp.where(i < s, i, i + 1)
    other = jnp.where(2 * s < shards, down, up)
    return jnp.where(i == shards - 1, s, other)


def greet(parts, shards, tensors):
    g, s, t = place()
    me = g * shards + s
    barrier = pltpu.get_barrier_semaphore()
    for i in range(1, parts):
        p = lax.rem(me + i, parts)
        pl.semaphore_signal(
            barrier, inc=1, device_id=(p // shards, lax.rem(p, shards), t), device_id_type=MESH
        )
    for m in range(1, tensors):
        pl.semaphore_signal(barrier, inc=1, device_id=(g, s, t ^ m), device_id_type=MESH)
    pl.semaphore_wait(barrier, parts + tensors - 2)


def bits(tensors):
    m, out = 1, []
    while m < tensors:
        out.append(m)
        m *= 2
    return out


def weight_columns(w_x, w_bc, d, shards):
    wide = w_x.shape[1] // shards
    group = d * (w_bc.shape[1] // (2 * STATE)) // shards
    return (
        w_x[:, pl.ds(pl.multiple_of(d * wide, 128), wide)],
        w_bc[:, pl.ds(pl.multiple_of(group * 2 * STATE, 128), 2 * STATE)],
    )


def one_hot(frame_row, s, rows):
    position = lax.broadcasted_iota(jnp.int32, (rows, 128), 0) + s * rows
    return jnp.where(position == frame_row, 1.0, 0.0).astype(F32)


def forward_kernel(
    shards, tensors, heads, tokens, ffeat, ids, w_proj, probe, w_x, w_bc, wdt,
    merged, proj, dts, prb, ids_out,
    turned, feats, outgo, cross, own, line, dt_part, dt_all, ff_all, ids_all, prb_all,
    a_s, a_r, f_s, f_r, h_s, h_r, x_s, x_r, z_s, z_r, d_s, d_r, e_s, e_r, i_s, i_r, b_s, b_r,
):
    parts = 2 * shards
    g, s, t = place()
    me = g * shards + s
    width = feats.shape[-1]
    sub = feats.shape[2]
    per = merged.shape[-1] // width
    count = shards * tensors * sub
    nq = proj.shape[0]
    span = shards // nq

    def peer(i):
        p = lax.rem(me + i, parts)
        return p, (p // shards, lax.rem(p, shards), t)

    greet(parts, shards, tensors)

    def seq_peer(i):
        return (g, lax.rem(s + i, shards), t)

    def send_ids(i):
        return rcopy(ids, ids_all.at[s], i_s.at[i], i_r.at[i], seq_peer(i))

    def send_ff(i):
        return rcopy(ffeat, ff_all.at[s], e_s.at[i], e_r.at[i], seq_peer(i))

    def send_probe(i):
        k = lax.rem(s + i, shards)
        wide = probe.shape[1] // shards
        at = pl.ds(pl.multiple_of(k * wide, 128), wide)
        return rcopy(probe.at[:, at], prb_all.at[s], b_s.at[i], b_r.at[i], seq_peer(i))

    for i in range(1, shards):
        send_ids(i).start()
        send_ff(i).start()
    ids_all[s] = ids[...]
    ff_all[s] = ffeat[...]
    for i in range(1, shards):
        k = lax.rem(s + shards - i, shards)
        rcopy(ids, ids_all.at[k], i_s.at[i], i_r.at[i], seq_peer(i)).wait_recv()
        rcopy(ffeat, ff_all.at[k], e_s.at[i], e_r.at[i], seq_peer(i)).wait_recv()
    frame_row = ids_all[0, 0:8]
    for k in range(1, shards):
        frame_row = jnp.maximum(frame_row, ids_all[k, 0:8])
    ids_out[0] = frame_row
    for k in range(shards):
        ids_out[1 + k] = ids_all[k, 8:16]
    slots = shards * ffeat.shape[0]
    emb = jnp.dot(
        ff_all[...].reshape(slots, ffeat.shape[1]), w_proj[...], preferred_element_type=F32
    ).astype(BF16)
    hot = one_hot(frame_row[0:1], s, tensors * sub)
    taken = jnp.sum(hot, axis=1, keepdims=True)
    placed = jnp.dot(hot[:, :slots].astype(BF16), emb, preferred_element_type=F32)
    for n in range(tensors):
        at = slice(n * sub, (n + 1) * sub)
        merged[n] = jnp.where(taken[at] > 0.5, placed[at], tokens[n].astype(F32)).astype(BF16)

    def turn(m):
        return rcopy(merged.at[t ^ m], turned.at[t], a_s.at[m], a_r.at[m], (g, s, t ^ m))

    for m in range(1, tensors):
        turn(m).start()
    turned[t] = merged[t]
    for m in range(1, tensors):
        rcopy(
            merged.at[t ^ m], turned.at[t ^ m], a_s.at[m], a_r.at[m], (g, s, t ^ m)
        ).wait_recv()

    def columns(r):
        return (r // per, slice(None), pl.ds(pl.multiple_of(lax.rem(r, per) * width, width), width))

    def spread(i):
        p, device = peer(i)
        return rcopy(turned.at[columns(p)], feats.at[me, t], f_s.at[i], f_r.at[i], device)

    for i in range(1, parts):
        spread(i).start()
    feats[me, t] = turned[columns(me)]
    for i in range(1, parts):
        q = lax.rem(me + parts - i, parts)
        p, device = peer(i)
        rcopy(feats.at[q, t], feats.at[q, t], f_s.at[i], f_r.at[i], device).wait_recv()

    def pass_on(gg, m, c, n):
        at = feats.at[pl.ds(gg * shards, shards), t ^ c]
        return rcopy(at, at, h_s.at[n, m | c], h_r.at[n, m | c], (g, s, t ^ m))

    def over_tensor(gg, n):
        held = [0]
        for m in reversed(bits(tensors)):
            for c in held:
                pass_on(gg, m, c, n).start()
            for c in held:
                at = feats.at[pl.ds(gg * shards, shards), t ^ (m | c)]
                rcopy(at, at, h_s.at[n, m | c], h_r.at[n, m | c], (g, s, t ^ m)).wait_recv()
            held = held + [m | c for c in held]

    over_tensor(1 - g, 0)

    def product(gg, d, q):
        rows = feats[pl.ds(gg * shards + q * span, span)].reshape(count // nq, width)
        for_x, for_bc = weight_columns(w_x, w_bc, d, shards)
        return jnp.concatenate(
            [
                jnp.dot(rows, for_x, preferred_element_type=F32).astype(BF16),
                jnp.dot(rows, for_bc, preferred_element_type=F32).astype(BF16),
            ],
            axis=1,
        )

    def to_cross(d, q):
        return rcopy(outgo.at[d, q], cross.at[d, q], x_s.at[d, q], x_r.at[d, q], (1 - g, s, t))

    def first(i, carry):
        d = far_first(i, s, shards)
        for q in range(nq):
            outgo[d, q] = product(1 - g, d, q)
            to_cross(d, q).start()
        return carry

    lax.fori_loop(0, shards, first, 0)
    for i in range(1, shards):
        send_probe(i).start()
    wide = probe.shape[1] // shards
    prb_all[s] = probe[:, pl.ds(pl.multiple_of(s * wide, 128), wide)]
    over_tensor(g, 1)

    for gg in range(2):
        rows = feats[gg * shards : (gg + 1) * shards].reshape(count, width)
        steps = lax.dot_general(
            wdt[...], rows, (((1,), (1,)), ((), ())), preferred_element_type=F32
        )
        for k in range(shards):
            dt_part[gg * shards + k] = steps[k * heads : (k + 1) * heads]

    def send_dt(i):
        p, device = peer(i)
        return rcopy(dt_part.at[p], dt_all.at[me], d_s.at[i], d_r.at[i], device)

    for i in range(1, parts):
        send_dt(i).start()
    dt_all[me] = dt_part[me]

    def right(d, q):
        return rcopy(own.at[d, q], line.at[d, q], z_s.at[d, q], z_r.at[d, q], (g, s + 1, t))

    def left(d, q):
        slot = jnp.where(d == s - 1, shards, d)
        return rcopy(own.at[d, q], line.at[slot, q], z_s.at[d, q], z_r.at[slot, q], (g, s - 1, t))

    def come(slot, q):
        rcopy(
            line.at[slot, q], line.at[slot, q], z_s.at[slot, q], z_r.at[slot, q], (1 - g, s, t)
        ).wait_recv()

    def second(i, carry):
        d = far_first(i, s, shards)
        for q in range(nq):
            own[d, q] = product(g, d, q)
        for q in range(nq):
            to_cross(d, q).wait_recv()
            has_more = ((d > s) & (s > 0)) | ((d < s) & (s < shards - 1))

            @pl.when(has_more)
            def _():
                come(d, q)
                own[d, q] = (
                    own[d, q].astype(F32) + cross[d, q].astype(F32) + line[d, q].astype(F32)
                ).astype(BF16)

            @pl.when(jnp.logical_not(has_more))
            def _():
                own[d, q] = (own[d, q].astype(F32) + cross[d, q].astype(F32)).astype(BF16)

            @pl.when(d > s)
            def _():
                right(d, q).start()

            @pl.when(d < s)
            def _():
                left(d, q).start()

        return carry

    lax.fori_loop(0, shards - 1, second, 0)
    for q in range(nq):
        own[s, q] = product(g, s, q)
    for q in range(nq):
        to_cross(s, q).wait_recv()
        own[s, q] = (own[s, q].astype(F32) + cross[s, q].astype(F32)).astype(BF16)

        @pl.when(s > 0)
        def _():
            come(s, q)
            own[s, q] = (own[s, q].astype(F32) + line[s, q].astype(F32)).astype(BF16)

        @pl.when(s < shards - 1)
        def _():
            come(shards, q)
            own[s, q] = (own[s, q].astype(F32) + line[shards, q].astype(F32)).astype(BF16)

        proj[q] = own[s, q]

    for i in range(1, parts):
        q = lax.rem(me + parts - i, parts)
        p, device = peer(i)
        rcopy(dt_part.at[p], dt_all.at[q], d_s.at[i], d_r.at[i], device).wait_recv()
    total = dt_all[0]
    for p in range(1, parts):
        total = total + dt_all[p]
    dts[...] = total

    for i in range(1, shards):
        k = lax.rem(s + shards - i, shards)
        rcopy(prb_all.at[k], prb_all.at[k], b_s.at[i], b_r.at[i], seq_peer(i)).wait_recv()
    prb[...] = prb_all[...]

    for i in range(1, shards):
        send_ids(i).wait_send()
        send_ff(i).wait_send()
        send_probe(i).wait_send()
    for m in range(1, tensors):
        turn(m).wait_send()
    for i in range(1, parts):
        spread(i).wait_send()
        send_dt(i).wait_send()
    for n, gg in enumerate((1 - g, g)):
        held = [0]
        for m in reversed(bits(tensors)):
            for c in held:
                pass_on(gg, m, c, n).wait_send()
            held = held + [m | c for c in held]

    def last(d, carry):
        for q in range(nq):
            to_cross(d, q).wait_send()

            @pl.when(d > s)
            def _():
                right(d, q).wait_send()

            @pl.when(d < s)
            def _():
                left(d, q).wait_send()

        return carry

    lax.fori_loop(0, shards, last, 0)


def forward(tokens, ffeat, ids, w_proj, probe, w_x, w_bc, wdt, shards, tensors, heads):
    parts = 2 * shards
    rows, held = tokens.shape
    sub = rows // tensors
    width = w_x.shape[0]
    wide = w_x.shape[1] // shards
    cols = wide + 2 * STATE
    count = rows * shards
    nq = 2
    block = (count // nq, cols)
    dma = pltpu.SemaphoreType.DMA
    merged, proj, dts, prb, ids_out = pl.pallas_call(
        functools.partial(forward_kernel, shards, tensors, heads),
        out_shape=(
            jax.ShapeDtypeStruct((tensors, sub, held), BF16),
            jax.ShapeDtypeStruct((nq,) + block, BF16),
            jax.ShapeDtypeStruct((heads, count), F32),
            jax.ShapeDtypeStruct((shards, rows, wide), BF16),
            jax.ShapeDtypeStruct((1 + shards, 8, 128), jnp.int32),
        ),
        in_specs=[pl.BlockSpec(memory_space=pltpu.VMEM)] * 8,
        out_specs=[pl.BlockSpec(memory_space=pltpu.VMEM)] * 5,
        scratch_shapes=[
            pltpu.VMEM((tensors, sub, held), BF16),
            pltpu.VMEM((parts, tensors, sub, width), BF16),
            pltpu.VMEM((shards, nq) + block, BF16),
            pltpu.VMEM((shards, nq) + block, BF16),
            pltpu.VMEM((shards, nq) + block, BF16),
            pltpu.VMEM((shards + 1, nq) + block, BF16),
            pltpu.VMEM((parts, heads, count), F32),
            pltpu.VMEM((parts, heads, count), F32),
            pltpu.VMEM((shards,) + ffeat.shape, BF16),
            pltpu.VMEM((shards,) + ids.shape, jnp.int32),
            pltpu.VMEM((shards, rows, wide), BF16),
            dma((tensors,)), dma((tensors,)),
            dma((parts,)), dma((parts,)),
            dma((2, tensors)), dma((2, tensors)),
            dma((shards, nq)), dma((shards, nq)),
            dma((shards + 1, nq)), dma((shards + 1, nq)),
            dma((parts,)), dma((parts,)),
            dma((shards,)), dma((shards,)),
            dma((shards,)), dma((shards,)),
            dma((shards,)), dma((shards,)),
        ],
        compiler_params=pltpu.CompilerParams(
            collective_id=0, has_side_effects=True, vmem_limit_bytes=VMEM_BYTES
        ),
        name="features_project_scatter",
    )(tokens.reshape(tensors, sub, held), ffeat, ids, w_proj, probe, w_x, w_bc, wdt)
    return merged, proj.reshape(count, cols), dts, prb.reshape(count, wide), ids_out


def running(x, back):
    count = x.shape[1]
    lane = lax.broadcasted_iota(jnp.int32, x.shape, 1)
    k = 1
    while k < count:
        if back:
            x = x + jnp.where(lane < count - k, pltpu.roll(x, count - k, 1), 0.0)
        else:
            x = x + jnp.where(lane >= k, pltpu.roll(x, k, 1), 0.0)
        k *= 2
    return x


def mixer_kernel(proj, raw, prb, seg_row, seg_col, params, grads, gdt, grad_c, row):
    heads, count = raw.shape
    wide = prb.shape[1]
    tall = 128
    shifted = raw[...] + params[:, 0:1]
    dt = jnp.maximum(shifted, 0.0) + jnp.log1p(jnp.exp(-jnp.abs(shifted)))
    ld = running(-dt * params[:, 1:2], False)
    dt_cols, ld_cols = dt.T, ld.T
    grad_c[...] = jnp.zeros_like(grad_c)
    row[...] = jnp.zeros_like(row)
    cols = []
    for start in range(0, count, tall):
        at, after = slice(start, start + tall), slice(start, count)
        span = count - start
        b = proj[at, wide : wide + STATE]
        c = proj[after, wide + STATE :]
        nt = (((1,), (1,)), ((), ()))
        scores = lax.dot_general(b, c, nt, preferred_element_type=F32)
        lane = lax.broadcasted_iota(jnp.int32, (tall, span), 1)
        line = lax.broadcasted_iota(jnp.int32, (tall, span), 0)
        visible = (seg_col[at] == seg_row[:, after]) & (lane >= line)
        grad_s = jnp.zeros((tall, span), F32)
        col = []
        for h in range(heads):
            here = slice(h * HEAD_DIM, (h + 1) * HEAD_DIM)
            p = prb[after, here]
            step = dt_cols[at, h : h + 1]
            gap = ld[h : h + 1, after] - ld_cols[at, h : h + 1]
            decay = jnp.exp(jnp.where(visible, gap, -1e30))
            paired = decay * lax.dot_general(
                proj[at, here], p, nt, preferred_element_type=F32
            )
            grad_s = grad_s + paired * step
            mixed = (decay * scores).astype(BF16)
            grad_x = jnp.dot(mixed, p, preferred_element_type=F32) * step
            grad_x = grad_x + params[h : h + 1, 2:3] * prb[at, here].astype(F32)
            grads[at, here] = grad_x.astype(BF16)
            weighted = paired * scores
            col.append(jnp.sum(weighted, axis=1, keepdims=True))
            row[h : h + 1, after] += jnp.sum(weighted * step, axis=0, keepdims=True)
        grad_s = grad_s.astype(BF16)
        grads[at, wide : wide + STATE] = jnp.dot(
            grad_s, c, preferred_element_type=F32
        ).astype(BF16)
        grad_c[after] += lax.dot_general(
            grad_s, b, (((0,), (0,)), ((), ())), preferred_element_type=F32
        )
        cols.append(jnp.concatenate(col, axis=1))
    grads[:, wide + STATE :] = grad_c[...].astype(BF16)
    col = jnp.concatenate(cols, axis=0).T
    later = running(row[...] - col * dt, True)
    gdt[...] = (col - params[:, 1:2] * later) / (1.0 + jnp.exp(-shifted))


def mixer(proj, raw, prb, seg, params):
    count, cols = proj.shape
    heads = raw.shape[0]
    return pl.pallas_call(
        mixer_kernel,
        out_shape=(
            jax.ShapeDtypeStruct((count, cols), BF16),
            jax.ShapeDtypeStruct((heads, count), F32),
        ),
        in_specs=[pl.BlockSpec(memory_space=pltpu.VMEM)] * 6,
        out_specs=[pl.BlockSpec(memory_space=pltpu.VMEM)] * 2,
        scratch_shapes=[pltpu.VMEM((count, STATE), F32), pltpu.VMEM((heads, count), F32)],
        compiler_params=pltpu.CompilerParams(vmem_limit_bytes=VMEM_BYTES),
        name="mixer_gradient",
    )(proj, raw, prb, seg[None, :], seg[:, None], params)


def backward_kernel(
    shards, tensors, merged, grads, gdt, w_x, w_bc, wdt, step, frame_row, adv, frames,
    every, dt_all, acc, back, halves, home, mine, tile, tiles_t, tiles_s, picked, given,
    x_s, x_r, z_s, z_r, d_s, d_r, r_s, r_r, h_s, h_r, m_s, m_r, p_s, p_r, q_s, q_r, g_s, g_r,
):
    parts = 2 * shards
    g, s, t = place()
    me = g * shards + s
    width = acc.shape[-1]
    sub = merged.shape[1]
    per = merged.shape[-1] // width
    count = shards * tensors * sub
    nq = grads.shape[0]
    span = shards // nq
    deep = tensors * sub

    def peer(i):
        p = lax.rem(me + i, parts)
        return p, (p // shards, lax.rem(p, shards), t)

    greet(parts, shards, tensors)

    def send_dt(i):
        p, device = peer(i)
        return rcopy(gdt, dt_all.at[me], d_s.at[i], d_r.at[i], device)

    def cross(j, q):
        return rcopy(every.at[g, j, q], every.at[g, j, q], x_s.at[j, q], x_r.at[j, q], (1 - g, s, t))

    def right(j, q):
        return rcopy(every.at[g, j, q], every.at[g, j, q], z_s.at[0, j, q], z_r.at[j, q], (g, s + 1, t))

    def left(j, q):
        return rcopy(every.at[g, j, q], every.at[g, j, q], z_s.at[1, j, q], z_r.at[j, q], (g, s - 1, t))

    def each_way(j, q, what):
        @pl.when((j <= s) & (s < shards - 1))
        def _():
            what(right(j, q))

        @pl.when((j >= s) & (s > 0))
        def _():
            what(left(j, q))

        what(cross(j, q))

    for q in range(nq):
        every[g, s, q] = grads[q]
        each_way(s, q, lambda c: c.start())
    for i in range(1, parts):
        send_dt(i).start()
    dt_all[me] = gdt[...]
    for i in range(1, parts):
        q = lax.rem(me + parts - i, parts)
        p, device = peer(i)
        rcopy(gdt, dt_all.at[q], d_s.at[i], d_r.at[i], device).wait_recv()
    for gg in range(2):
        stack = jnp.concatenate([dt_all[gg * shards + k] for k in range(shards)], axis=0)
        acc[gg] = jnp.dot(
            stack.T.astype(BF16), wdt[...], preferred_element_type=F32
        ).reshape(nq, count // nq, width)

    def add(gg, j, q):
        for_x, for_bc = weight_columns(w_x, w_bc, j, shards)
        wide = for_x.shape[1]
        nt = (((1,), (1,)), ((), ()))
        acc[gg, q] += lax.dot_general(
            every[gg, j, q, :, :wide], for_x, nt, preferred_element_type=F32
        ) + lax.dot_general(
            every[gg, j, q, :, wide:], for_bc, nt, preferred_element_type=F32
        )

    def add_cross(j, q):
        rcopy(
            every.at[1 - g, j, q], every.at[1 - g, j, q], x_s.at[j, q], x_r.at[j, q], (1 - g, s, t)
        ).wait_recv()
        add(1 - g, j, q)

    for q in range(nq):
        add(g, s, q)

    def lap(i, carry):
        j = far_first(shards - 1 - i, s, shards)
        before = far_first(shards - i, s, shards)
        for q in range(nq):
            rcopy(
                every.at[g, j, q], every.at[g, j, q], x_s.at[j, q], z_r.at[j, q], (1 - g, s, t)
            ).wait_recv()
            each_way(j, q, lambda c: c.start())
            add(g, j, q)
            add_cross(before, q)
        return carry

    lax.fori_loop(1, shards, lap, 0)

    steps = bits(tensors)

    def reduce_tensor(gg):
        for c in range(shards):
            q, k = c // span, c % span
            back[gg, c] = (
                acc[gg, q, k * deep : (k + 1) * deep].astype(BF16).reshape(tensors, sub, width)
            )
        low, size = 0, tensors
        for n, m in enumerate(steps):
            size //= 2
            bit = lax.rem(t // m, 2)
            keep, give = low + bit * size, low + (1 - bit) * size
            at = tensors - 2 * size
            copy = rcopy(
                back.at[gg, :, pl.ds(give, size)], halves.at[gg, :, pl.ds(at, size)],
                r_s.at[gg, n], r_r.at[gg, n], (g, s, t ^ m),
            )
            copy.start()
            copy.wait_recv()
            back[gg, :, pl.ds(keep, size)] = (
                back[gg, :, pl.ds(keep, size)].astype(F32)
                + halves[gg, :, at : at + size].astype(F32)
            ).astype(BF16)
            copy.wait_send()
            low = keep
        return low

    def send_home(gg, k):
        return rcopy(
            back.at[gg, k, spot], home.at[me], h_s.at[gg * shards + k], h_r.at[me], (gg, k, t)
        )

    spot = reduce_tensor(g)
    for k in range(shards):
        @pl.when(k != s)
        def _():
            send_home(g, k).start()

    home[me] = back[g, s, spot]
    last = far_first(0, s, shards)
    for q in range(nq):
        add_cross(last, q)
    spot = reduce_tensor(1 - g)
    for k in range(shards):
        send_home(1 - g, k).start()
    for i in range(1, parts):
        p, device = peer(i)
        rcopy(home.at[p], home.at[p], h_s.at[p], h_r.at[p], device).wait_recv()

    def turn(m):
        at = pl.ds((t ^ m) * per, per)
        return rcopy(home.at[at], mine.at[spot], m_s.at[m], m_r.at[m], (g, s, t ^ m))

    def spot_of(tt):
        low, size = 0, tensors
        for m in steps:
            size //= 2
            low = low + lax.rem(tt // m, 2) * size
        return low

    for m in range(1, tensors):
        turn(m).start()
    mine[spot] = home[pl.ds(t * per, per)]
    for m in range(1, tensors):
        at = spot_of(t ^ m)
        rcopy(mine.at[at], mine.at[at], m_s.at[m], m_r.at[m], (g, s, t ^ m)).wait_recv()

    total = jnp.zeros((8, 128), F32)
    for n in range(tensors):
        for h in range(per):
            sq = mine[n, h].astype(F32)
            sq = jnp.sum((sq * sq).reshape(sub // 8, 8, width), axis=0)
            for b in range(width // 128):
                total = total + sq[:, b * 128 : (b + 1) * 128]
    tile[0] = total

    def share_t(m):
        return rcopy(tile.at[0], tiles_t.at[m], p_s.at[m], p_r.at[m], (g, s, t ^ m))

    for m in range(1, tensors):
        share_t(m).start()
    for m in range(1, tensors):
        share_t(m).wait_recv()
        total = total + tiles_t[m]
    tile[1] = total

    def share_s(i):
        return rcopy(
            tile.at[1], tiles_s.at[i], q_s.at[i], q_r.at[i], (g, lax.rem(s + i, shards), t)
        )

    for i in range(1, shards):
        share_s(i).start()
    for i in range(1, shards):
        share_s(i).wait_recv()
        total = total + tiles_s[i]
    entries = count * parts * width
    scale = lax.rsqrt(jnp.sum(total, keepdims=True) / entries + 1e-06)
    for n in range(tensors):
        move = step[n] * scale
        for h in range(per):
            at = slice(h * width, (h + 1) * width)
            adv[n, :, at] = (
                merged[n, :, at].astype(F32) + move * mine[n, h].astype(F32)
            ).astype(BF16)

    slots = picked.shape[1]
    hot = one_hot(frame_row[0:1], s, deep).T[: shards * slots].astype(BF16)
    chosen = jnp.dot(hot, adv[...].reshape(deep, -1), preferred_element_type=F32)
    picked[...] = chosen.astype(BF16).reshape(picked.shape)

    def give_back(i):
        k = lax.rem(s + i, shards)
        return rcopy(picked.at[k], given.at[i], g_s.at[i], g_r.at[i], (g, k, t))

    for i in range(1, shards):
        give_back(i).start()
    total = picked[s].astype(F32)
    for i in range(1, shards):
        give_back(i).wait_recv()
        total = total + given[i].astype(F32)
    frames[...] = total.astype(BF16)

    for i in range(1, parts):
        send_dt(i).wait_send()
    for m in range(1, tensors):
        turn(m).wait_send()
        share_t(m).wait_send()
    for i in range(1, shards):
        share_s(i).wait_send()
        give_back(i).wait_send()
    for k in range(shards):
        @pl.when(k != s)
        def _():
            send_home(g, k).wait_send()

        send_home(1 - g, k).wait_send()

    def end(j, carry):
        for q in range(nq):
            each_way(j, q, lambda c: c.wait_send())
        return carry

    lax.fori_loop(0, shards, end, 0)


def backward(merged, grads, gdt, w_x, w_bc, wdt, direction, frame_row, slots, shards):
    parts = 2 * shards
    tensors, sub, held = merged.shape
    rows = tensors * sub
    width = w_x.shape[0]
    cols = grads.shape[1]
    count = rows * shards
    per = held // width
    heads = gdt.shape[0]
    nq = 2
    block = (count // nq, cols)
    dma = pltpu.SemaphoreType.DMA
    levels = len(bits(tensors))
    adv, frames = pl.pallas_call(
        functools.partial(backward_kernel, shards, tensors),
        out_shape=(
            jax.ShapeDtypeStruct((tensors, sub, held), BF16),
            jax.ShapeDtypeStruct((slots, held), BF16),
        ),
        in_specs=[pl.BlockSpec(memory_space=pltpu.VMEM)] * 8,
        out_specs=[pl.BlockSpec(memory_space=pltpu.VMEM)] * 2,
        scratch_shapes=[
            pltpu.VMEM((2, shards, nq) + block, BF16),
            pltpu.VMEM((parts, heads, count), F32),
            pltpu.VMEM((2, nq, count // nq, width), F32),
            pltpu.VMEM((2, shards, tensors, sub, width), BF16),
            pltpu.VMEM((2, shards, tensors, sub, width), BF16),
            pltpu.VMEM((parts, sub, width), BF16),
            pltpu.VMEM((tensors, per, sub, width), BF16),
            pltpu.VMEM((2, 8, 128), F32),
            pltpu.VMEM((tensors, 8, 128), F32),
            pltpu.VMEM((shards, 8, 128), F32),
            pltpu.VMEM((shards, slots, held), BF16),
            pltpu.VMEM((shards, slots, held), BF16),
            dma((shards, nq)), dma((shards, nq)),
            dma((2, shards, nq)), dma((shards, nq)),
            dma((parts,)), dma((parts,)),
            dma((2, levels)), dma((2, levels)),
            dma((parts,)), dma((parts,)),
            dma((tensors,)), dma((tensors,)),
            dma((tensors,)), dma((tensors,)),
            dma((shards,)), dma((shards,)),
            dma((shards,)), dma((shards,)),
        ],
        compiler_params=pltpu.CompilerParams(
            collective_id=1, has_side_effects=True, vmem_limit_bytes=VMEM_BYTES
        ),
        name="gather_project_step",
    )(
        merged,
        grads.reshape((nq,) + block),
        gdt,
        w_x,
        w_bc,
        wdt,
        direction.reshape(tensors, sub, 1),
        frame_row,
    )
    return adv.reshape(rows, held), frames


def in_vmem(groups, shards, tensors, rows, width, cols, slots):
    if groups != 2 or shards % 2 or tensors & (tensors - 1) or rows % (16 * tensors):
        return False
    if rows != 128 or slots * shards > 128:
        return False
    if width % 128 or cols % 128 or shards * width * 2 % tensors:
        return False
    count = rows * shards
    lines = 2 * count * cols * (4 * shards + 1)
    sums = 2 * count * width * 4 + 4 * count * cols * shards
    return max(lines, sums) + 2 * width * cols * shards + 8 * count * width < VMEM_BYTES // 2


def mixer_grad(x, b, c, pdt, probe, seg, dt_bias, decay_rate, skip_gain):
    count, heads = pdt.shape
    shifted = pdt + dt_bias[None, :]
    dt = jax.nn.softplus(shifted).T
    ld = jnp.cumsum(-dt * decay_rate[:, None], axis=1)
    position = jnp.arange(count)
    visible = (seg[:, None] == seg[None, :]) & (position[:, None] >= position[None, :])
    gap = ld[:, :, None] - ld[:, None, :]
    decay = jnp.where(visible[None], jnp.exp(jnp.where(visible[None], gap, 0.0)), 0.0)
    xh = x.astype(BF16).reshape(count, heads, HEAD_DIM)
    ph = probe.reshape(count, heads, HEAD_DIM)
    bb, cb = b.astype(BF16), c.astype(BF16)
    scores = jnp.dot(cb, bb.T, preferred_element_type=F32)
    pairs = jnp.einsum("thp,shp->hts", ph, xh, preferred_element_type=F32)
    mixed = decay * scores[None]
    grad_x = jnp.einsum("hts,thp->shp", mixed.astype(BF16), ph, preferred_element_type=F32)
    grad_x = grad_x * dt.T[:, :, None] + skip_gain[None, :, None] * ph.astype(F32)
    weighted = mixed * pairs
    col = jnp.sum(weighted, axis=1)
    row = jnp.sum(weighted * dt[:, None, :], axis=2)
    grad_s = jnp.sum(decay * pairs * dt[:, None, :], axis=0).astype(BF16)
    grad_c = jnp.dot(grad_s, bb, preferred_element_type=F32)
    grad_b = jnp.dot(grad_s.T, cb, preferred_element_type=F32)
    grad_ld = row - col * dt
    later = jnp.cumsum(grad_ld[:, ::-1], axis=1)[:, ::-1]
    grad_dt = (col - decay_rate[:, None] * later).T * jax.nn.sigmoid(shifted)
    return grad_x.reshape(count, -1), grad_b, grad_c, grad_dt


def by_collectives(
    tokens,
    frame_feats,
    w_proj,
    frame_pos,
    segments,
    signs,
    w_x,
    w_bc,
    w_dt,
    dt_bias,
    decay_rate,
    skip_gain,
    probe,
):
    rows = tokens.shape[1]
    groups, shards, tensors = (lax.axis_size(a) for a in ("group", "seq", "tensor"))
    g, s, t = (lax.axis_index(a) for a in ("group", "seq", "tensor"))
    parts = groups * shards
    count = rows * shards
    width = w_x.shape[0]
    heads = w_dt.shape[1] // shards
    per_group = w_dt.shape[1] * 2 * STATE // w_bc.shape[1]
    cols_x = heads * HEAD_DIM
    group_of = [(k * heads) // per_group for k in range(shards)]
    cols = cols_x + 2 * STATE + heads

    feats, pos = (
        lax.all_to_all(frame_feats[0], "seq", split_axis=0, concat_axis=0, tiled=True),
        lax.all_to_all(frame_pos[0], "seq", split_axis=0, concat_axis=0, tiled=True),
    )
    local_pos = pos - s * rows
    arrived = jnp.dot(feats, w_proj, preferred_element_type=F32).astype(BF16)
    merged = tokens[0].at[local_pos].set(arrived)

    sub = rows // tensors
    f = lax.all_to_all(merged, "tensor", split_axis=0, concat_axis=1, tiled=True)
    f = f.reshape(sub, parts, width).transpose(1, 0, 2)
    f = lax.all_to_all(f, ("group", "seq"), split_axis=0, concat_axis=0, tiled=True)
    f = lax.all_gather(f, "tensor", axis=1, tiled=True)
    f = f.reshape(groups, count, width)

    weights = jnp.stack(
        [
            jnp.concatenate(
                [
                    w_x[:, k * cols_x : (k + 1) * cols_x],
                    w_bc[:, group_of[k] * 2 * STATE : (group_of[k] + 1) * 2 * STATE],
                    w_dt[:, k * heads : (k + 1) * heads],
                ],
                axis=1,
            )
            for k in range(shards)
        ]
    )
    partial = jnp.einsum("gtk,skc->gstc", f, weights, preferred_element_type=F32).astype(BF16)
    proj = lax.psum_scatter(
        partial.reshape(parts, count, cols), ("group", "seq"), scatter_dimension=0, tiled=False
    ).astype(F32)

    seg = lax.all_gather(segments[0], "seq", axis=0, tiled=True)
    prb = lax.all_to_all(
        probe[0].reshape(rows, shards, cols_x).transpose(1, 0, 2),
        "seq",
        split_axis=0,
        concat_axis=0,
        tiled=True,
    ).reshape(count, cols_x)

    def own(v):
        return lax.dynamic_slice(v, (s * heads,), (heads,))

    grads = mixer_grad(
        proj[:, :cols_x],
        proj[:, cols_x : cols_x + STATE],
        proj[:, cols_x + STATE : cols_x + 2 * STATE],
        proj[:, cols_x + 2 * STATE :],
        prb,
        seg,
        own(dt_bias),
        own(decay_rate),
        own(skip_gain),
    )
    grads = jnp.concatenate([v.astype(BF16) for v in grads], axis=1)
    every = lax.all_gather(grads, ("group", "seq"), axis=0, tiled=False)
    every = every.reshape(groups, shards, count, cols)
    back = jnp.einsum("gstc,skc->gtk", every, weights, preferred_element_type=F32).astype(BF16)

    back = back.reshape(parts, tensors, sub, width).transpose(1, 0, 2, 3)
    back = lax.all_to_all(back, "tensor", split_axis=0, concat_axis=0, tiled=True)
    summed = jnp.sum(back.astype(F32), axis=0)
    squares = jnp.sum(summed.reshape(groups, -1) ** 2, axis=1)
    squares = lax.psum(squares, ("group", "seq", "tensor"))[g]
    home = lax.all_to_all(
        summed.astype(BF16), ("group", "seq"), split_axis=0, concat_axis=0, tiled=True
    )
    home = home.transpose(1, 0, 2).reshape(sub, tensors, -1).transpose(1, 0, 2)
    gradient = lax.all_to_all(home, "tensor", split_axis=0, concat_axis=0, tiled=True)
    gradient = gradient.reshape(rows, -1).astype(F32)

    entries = count * parts * width
    grad_scale = jnp.sqrt(squares / entries + 1e-06)
    direction = (2 * signs[0] - 1).astype(F32)[:, None]
    adv = (merged.astype(F32) + 0.5 * direction * gradient / grad_scale).astype(BF16)
    picked = adv[local_pos]
    returned = lax.all_to_all(picked, "seq", split_axis=0, concat_axis=0, tiled=True)
    return (adv[None], returned[None])


def body(*arrays):
    tokens, frame_feats, w_x, w_dt = arrays[0], arrays[1], arrays[6], arrays[8]
    sizes = tuple(lax.axis_size(a) for a in ("group", "seq", "tensor"))
    cols = w_dt.shape[1] // sizes[1] * HEAD_DIM + 2 * STATE
    slots = -(-frame_feats.shape[1] // 16) * 16
    if in_vmem(*sizes, tokens.shape[1], w_x.shape[0], cols, slots):
        return by_kernels(slots, *arrays)
    return by_collectives(*arrays)


def by_kernels(
    slots,
    tokens,
    frame_feats,
    w_proj,
    frame_pos,
    segments,
    signs,
    w_x,
    w_bc,
    w_dt,
    dt_bias,
    decay_rate,
    skip_gain,
    probe,
):
    shards, tensors = lax.axis_size("seq"), lax.axis_size("tensor")
    s = lax.axis_index("seq")
    frames = frame_feats.shape[1]
    heads = w_dt.shape[1] // shards
    ffeat = jnp.pad(frame_feats[0], ((0, slots - frames), (0, 0)))
    lane = jnp.full((shards, slots), -1, jnp.int32)
    lane = lax.dynamic_update_slice(lane, frame_pos, (s, 0)).reshape(1, -1)
    lane = jnp.pad(lane, ((0, 0), (0, 128 - shards * slots)), constant_values=-1)
    ids = jnp.concatenate([jnp.broadcast_to(v, (8, 128)) for v in (lane, segments)], axis=0)
    w_step = w_dt.T
    merged, proj, raw, prb, ids = forward(
        tokens[0], ffeat, ids, w_proj, probe[0], w_x, w_bc, w_step, shards, tensors, heads
    )
    params = jnp.stack([dt_bias, decay_rate, skip_gain], axis=1)
    params = lax.dynamic_slice(params, (s * heads, 0), (heads, 3))
    grads, gdt = mixer(proj, raw, prb, ids[1:, 0].reshape(-1), params)
    direction = 0.5 * (2 * signs[0] - 1).astype(F32)
    adv, returned = backward(
        merged, grads, gdt, w_x, w_bc, w_step, direction, ids[0], slots, shards
    )
    return (adv[None], returned[None, :frames])


def solution(mesh):
    return jax.shard_map(
        body,
        mesh=mesh,
        in_specs=(
            P("group", "seq", "tensor"),
            P("group", "seq", None),
            P(None, "tensor"),
            P("group", "seq"),
            P("group", "seq"),
            P("group", "seq"),
            P(("group", "seq"), "tensor"),
            P(("group", "seq"), "tensor"),
            P(("group", "seq"), "tensor"),
            P("tensor"),
            P("tensor"),
            P("tensor"),
            P("group", "seq", "tensor"),
        ),
        out_specs=(P("group", "seq", "tensor"), P("group", "seq", "tensor")),
        check_vma=False,
    )
```

```python
import functools

import jax
import jax.numpy as jnp
from jax import lax
from jax.experimental import pallas as pl
from jax.experimental.pallas import tpu as pltpu
from jax.sharding import PartitionSpec as P

HEAD_DIM = 64
STATE = 128
BF16 = jnp.bfloat16
F32 = jnp.float32


MESH = pl.DeviceIdType.MESH
VMEM_BYTES = 58 * 2**20


def place():
    return tuple(lax.axis_index(a) for a in ("group", "seq", "tensor"))


def rcopy(src, dst, send, recv, device):
    return pltpu.make_async_remote_copy(
        src_ref=src, dst_ref=dst, send_sem=send, recv_sem=recv, device_id=device, device_id_type=MESH
    )


def far_first(i, s, shards):
    down = jnp.where(i < shards - 1 - s, shards - 1 - i, shards - 2 - i)
    up = jnp.where(i < s, i, i + 1)
    other = jnp.where(2 * s < shards, down, up)
    return jnp.where(i == shards - 1, s, other)


def greet(parts, shards, tensors):
    g, s, t = place()
    me = g * shards + s
    barrier = pltpu.get_barrier_semaphore()
    for i in range(1, parts):
        p = lax.rem(me + i, parts)
        pl.semaphore_signal(
            barrier, inc=1, device_id=(p // shards, lax.rem(p, shards), t), device_id_type=MESH
        )
    for m in range(1, tensors):
        pl.semaphore_signal(barrier, inc=1, device_id=(g, s, t ^ m), device_id_type=MESH)
    pl.semaphore_wait(barrier, parts + tensors - 2)


def bits(tensors):
    m, out = 1, []
    while m < tensors:
        out.append(m)
        m *= 2
    return out


def columns_of(w, k, wide):
    return w[:, pl.ds(pl.multiple_of(k * wide, 128), wide)]


def one_hot(frame_row, s, rows):
    position = lax.broadcasted_iota(jnp.int32, (rows, 128), 0) + s * rows
    return jnp.where(position == frame_row, 1.0, 0.0).astype(F32)


def forward_kernel(
    shards, tensors, heads, tokens, ffeat, ids, w_proj_hbm, probe, w_x_hbm, w_bc_hbm, wdt,
    merged, proj, dts, prb, ids_out,
    w_proj, w_x, w_bc, turned, feats, outgo, cross, out_bc, cross_bc, own, line, dt_part, dt_all, ff_all, ids_all, prb_all,
    a_s, a_r, f_s, f_r, h_s, h_r, x_s, x_r, z_s, z_r, d_s, d_r, e_s, e_r, i_s, i_r, b_s, b_r, c_s, c_r, w_sem,
):
    parts = 2 * shards
    g, s, t = place()
    me = g * shards + s
    width = feats.shape[-1]
    sub = feats.shape[2]
    per = merged.shape[-1] // width
    count = shards * tensors * sub
    nq = proj.shape[0]
    span = shards // nq

    def peer(i):
        p = lax.rem(me + i, parts)
        return p, (p // shards, lax.rem(p, shards), t)

    loads = [
        pltpu.make_async_copy(src, dst, w_sem.at[n])
        for n, (src, dst) in enumerate(((w_proj_hbm, w_proj), (w_x_hbm, w_x), (w_bc_hbm, w_bc)))
    ]
    for load in loads:
        load.start()
    wide = w_x.shape[1] // shards
    pairs = shards // (w_bc.shape[1] // (2 * STATE))
    greet(parts, shards, tensors)

    def seq_peer(i):
        return (g, lax.rem(s + i, shards), t)

    def send_ids(i):
        return rcopy(ids, ids_all.at[s], i_s.at[i], i_r.at[i], seq_peer(i))

    def send_ff(i):
        return rcopy(ffeat, ff_all.at[s], e_s.at[i], e_r.at[i], seq_peer(i))

    def send_probe(i):
        k = lax.rem(s + i, shards)
        wide = probe.shape[1] // shards
        at = pl.ds(pl.multiple_of(k * wide, 128), wide)
        return rcopy(probe.at[:, at], prb_all.at[s], b_s.at[i], b_r.at[i], seq_peer(i))

    for i in range(1, shards):
        send_ids(i).start()
        send_ff(i).start()
    ids_all[s] = ids[...]
    ff_all[s] = ffeat[...]
    for i in range(1, shards):
        k = lax.rem(s + shards - i, shards)
        rcopy(ids, ids_all.at[k], i_s.at[i], i_r.at[i], seq_peer(i)).wait_recv()
        rcopy(ffeat, ff_all.at[k], e_s.at[i], e_r.at[i], seq_peer(i)).wait_recv()
    frame_row = ids_all[0, 0:8]
    for k in range(1, shards):
        frame_row = jnp.maximum(frame_row, ids_all[k, 0:8])
    ids_out[0] = frame_row
    for k in range(shards):
        ids_out[1 + k] = ids_all[k, 8:16]
    slots = shards * ffeat.shape[0]
    loads[0].wait()
    emb = jnp.dot(
        ff_all[...].reshape(slots, ffeat.shape[1]), w_proj[...], preferred_element_type=F32
    ).astype(BF16)
    hot = one_hot(frame_row[0:1], s, tensors * sub)
    taken = jnp.sum(hot, axis=1, keepdims=True)
    placed = jnp.dot(hot[:, :slots].astype(BF16), emb, preferred_element_type=F32)
    for n in range(tensors):
        at = slice(n * sub, (n + 1) * sub)
        merged[n] = jnp.where(taken[at] > 0.5, placed[at], tokens[n].astype(F32)).astype(BF16)

    def turn(m):
        return rcopy(merged.at[t ^ m], turned.at[t], a_s.at[m], a_r.at[m], (g, s, t ^ m))

    for m in range(1, tensors):
        turn(m).start()
    turned[t] = merged[t]
    for m in range(1, tensors):
        rcopy(
            merged.at[t ^ m], turned.at[t ^ m], a_s.at[m], a_r.at[m], (g, s, t ^ m)
        ).wait_recv()

    def columns(r):
        return (r // per, slice(None), pl.ds(pl.multiple_of(lax.rem(r, per) * width, width), width))

    def spread(i):
        p, device = peer(i)
        return rcopy(turned.at[columns(p)], feats.at[me, t], f_s.at[i], f_r.at[i], device)

    for i in range(1, parts):
        spread(i).start()
    feats[me, t] = turned[columns(me)]
    for i in range(1, parts):
        q = lax.rem(me + parts - i, parts)
        p, device = peer(i)
        rcopy(feats.at[q, t], feats.at[q, t], f_s.at[i], f_r.at[i], device).wait_recv()

    def pass_on(gg, m, c, n):
        at = feats.at[pl.ds(gg * shards, shards), t ^ c]
        return rcopy(at, at, h_s.at[n, m | c], h_r.at[n, m | c], (g, s, t ^ m))

    def over_tensor(gg, n):
        held = [0]
        for m in reversed(bits(tensors)):
            for c in held:
                pass_on(gg, m, c, n).start()
            for c in held:
                at = feats.at[pl.ds(gg * shards, shards), t ^ (m | c)]
                rcopy(at, at, h_s.at[n, m | c], h_r.at[n, m | c], (g, s, t ^ m)).wait_recv()
            held = held + [m | c for c in held]

    over_tensor(1 - g, 0)

    def product(gg, q, w):
        rows = feats[pl.ds(gg * shards + q * span, span)].reshape(count // nq, width)
        return jnp.dot(rows, w, preferred_element_type=F32).astype(BF16)

    def for_x(gg, d, q):
        return product(gg, q, columns_of(w_x, d, wide))

    def for_bc(gg, d, q):
        return product(gg, q, columns_of(w_bc, d // pairs, 2 * STATE))

    def to_cross(d, q):
        return rcopy(outgo.at[d, q], cross.at[d, q], x_s.at[d, q], x_r.at[d, q], (1 - g, s, t))

    def bc_to_cross(d, q):
        n = d // pairs
        return rcopy(out_bc.at[n, q], cross_bc.at[n, q], c_s.at[n, q], c_r.at[n, q], (1 - g, s, t))

    loads[1].wait()
    loads[2].wait()

    def first(i, carry):
        d = far_first(i, s, shards)
        for q in range(nq):
            outgo[d, q] = for_x(1 - g, d, q)
            to_cross(d, q).start()

            @pl.when(lax.rem(i, pairs) == 0)
            def _():
                out_bc[d // pairs, q] = for_bc(1 - g, d, q)
                bc_to_cross(d, q).start()

        return carry

    lax.fori_loop(0, shards, first, 0)
    for i in range(1, shards):
        send_probe(i).start()
    prb_all[s] = probe[:, pl.ds(pl.multiple_of(s * wide, 128), wide)]
    over_tensor(g, 1)

    for gg in range(2):
        rows = feats[gg * shards : (gg + 1) * shards].reshape(count, width)
        steps = lax.dot_general(
            wdt[...], rows, (((1,), (1,)), ((), ())), preferred_element_type=F32
        )
        for k in range(shards):
            dt_part[gg * shards + k] = steps[k * heads : (k + 1) * heads]

    def send_dt(i):
        p, device = peer(i)
        return rcopy(dt_part.at[p], dt_all.at[me], d_s.at[i], d_r.at[i], device)

    for i in range(1, parts):
        send_dt(i).start()
    dt_all[me] = dt_part[me]

    def right(d, q):
        return rcopy(own.at[d, q], line.at[d, q], z_s.at[d, q], z_r.at[d, q], (g, s + 1, t))

    def left(d, q):
        slot = jnp.where(d == s - 1, shards, d)
        return rcopy(own.at[d, q], line.at[slot, q], z_s.at[d, q], z_r.at[slot, q], (g, s - 1, t))

    def come(slot, q):
        rcopy(
            line.at[slot, q], line.at[slot, q], z_s.at[slot, q], z_r.at[slot, q], (1 - g, s, t)
        ).wait_recv()

    def both_samples(d, q):
        mine_x = own[d, q, :, :wide].astype(F32) + cross[d, q].astype(F32)
        mine_bc = own[d, q, :, wide:].astype(F32) + cross_bc[d // pairs, q].astype(F32)
        return jnp.concatenate([mine_x, mine_bc], axis=1)

    def second(i, carry):
        d = far_first(i, s, shards)
        for q in range(nq):
            own[d, q, :, :wide] = for_x(g, d, q)
            own[d, q, :, wide:] = for_bc(g, d, q)
        for q in range(nq):
            to_cross(d, q).wait_recv()

            @pl.when(lax.rem(i, pairs) == 0)
            def _():
                bc_to_cross(d, q).wait_recv()

            has_more = ((d > s) & (s > 0)) | ((d < s) & (s < shards - 1))

            @pl.when(has_more)
            def _():
                come(d, q)
                own[d, q] = (both_samples(d, q) + line[d, q].astype(F32)).astype(BF16)

            @pl.when(jnp.logical_not(has_more))
            def _():
                own[d, q] = both_samples(d, q).astype(BF16)

            @pl.when(d > s)
            def _():
                right(d, q).start()

            @pl.when(d < s)
            def _():
                left(d, q).start()

        return carry

    lax.fori_loop(0, shards - 1, second, 0)
    for q in range(nq):
        own[s, q, :, :wide] = for_x(g, s, q)
        own[s, q, :, wide:] = for_bc(g, s, q)
    for q in range(nq):
        to_cross(s, q).wait_recv()
        own[s, q] = both_samples(s, q).astype(BF16)

        @pl.when(s > 0)
        def _():
            come(s, q)
            own[s, q] = (own[s, q].astype(F32) + line[s, q].astype(F32)).astype(BF16)

        @pl.when(s < shards - 1)
        def _():
            come(shards, q)
            own[s, q] = (own[s, q].astype(F32) + line[shards, q].astype(F32)).astype(BF16)

        proj[q] = own[s, q]

    for i in range(1, parts):
        q = lax.rem(me + parts - i, parts)
        p, device = peer(i)
        rcopy(dt_part.at[p], dt_all.at[q], d_s.at[i], d_r.at[i], device).wait_recv()
    total = dt_all[0]
    for p in range(1, parts):
        total = total + dt_all[p]
    dts[...] = total

    for i in range(1, shards):
        k = lax.rem(s + shards - i, shards)
        rcopy(prb_all.at[k], prb_all.at[k], b_s.at[i], b_r.at[i], seq_peer(i)).wait_recv()
    prb[...] = prb_all[...]

    for i in range(1, shards):
        send_ids(i).wait_send()
        send_ff(i).wait_send()
        send_probe(i).wait_send()
    for m in range(1, tensors):
        turn(m).wait_send()
    for i in range(1, parts):
        spread(i).wait_send()
        send_dt(i).wait_send()
    for n, gg in enumerate((1 - g, g)):
        held = [0]
        for m in reversed(bits(tensors)):
            for c in held:
                pass_on(gg, m, c, n).wait_send()
            held = held + [m | c for c in held]

    def last(d, carry):
        for q in range(nq):
            to_cross(d, q).wait_send()

            @pl.when(lax.rem(d, pairs) == 0)
            def _():
                bc_to_cross(d, q).wait_send()

            @pl.when(d > s)
            def _():
                right(d, q).wait_send()

            @pl.when(d < s)
            def _():
                left(d, q).wait_send()

        return carry

    lax.fori_loop(0, shards, last, 0)


def forward(tokens, ffeat, ids, w_proj, probe, w_x, w_bc, wdt, shards, tensors, heads):
    parts = 2 * shards
    rows, held = tokens.shape
    sub = rows // tensors
    width = w_x.shape[0]
    wide = w_x.shape[1] // shards
    maps = w_bc.shape[1] // (2 * STATE)
    cols = wide + 2 * STATE
    count = rows * shards
    nq = 2
    block = (count // nq, cols)
    dma = pltpu.SemaphoreType.DMA
    merged, proj, dts, prb, ids_out = pl.pallas_call(
        functools.partial(forward_kernel, shards, tensors, heads),
        out_shape=(
            jax.ShapeDtypeStruct((tensors, sub, held), BF16),
            jax.ShapeDtypeStruct((nq,) + block, BF16),
            jax.ShapeDtypeStruct((heads, count), F32),
            jax.ShapeDtypeStruct((shards, rows, wide), BF16),
            jax.ShapeDtypeStruct((1 + shards, 8, 128), jnp.int32),
        ),
        in_specs=[
            pl.BlockSpec(memory_space=pl.ANY if n in (3, 5, 6) else pltpu.VMEM) for n in range(8)
        ],
        out_specs=[pl.BlockSpec(memory_space=pltpu.VMEM)] * 5,
        scratch_shapes=[
            pltpu.VMEM(w_proj.shape, BF16),
            pltpu.VMEM(w_x.shape, BF16),
            pltpu.VMEM(w_bc.shape, BF16),
            pltpu.VMEM((tensors, sub, held), BF16),
            pltpu.VMEM((parts, tensors, sub, width), BF16),
            pltpu.VMEM((shards, nq, count // nq, wide), BF16),
            pltpu.VMEM((shards, nq, count // nq, wide), BF16),
            pltpu.VMEM((maps, nq, count // nq, 2 * STATE), BF16),
            pltpu.VMEM((maps, nq, count // nq, 2 * STATE), BF16),
            pltpu.VMEM((shards, nq) + block, BF16),
            pltpu.VMEM((shards + 1, nq) + block, BF16),
            pltpu.VMEM((parts, heads, count), F32),
            pltpu.VMEM((parts, heads, count), F32),
            pltpu.VMEM((shards,) + ffeat.shape, BF16),
            pltpu.VMEM((shards,) + ids.shape, jnp.int32),
            pltpu.VMEM((shards, rows, wide), BF16),
            dma((tensors,)), dma((tensors,)),
            dma((parts,)), dma((parts,)),
            dma((2, tensors)), dma((2, tensors)),
            dma((shards, nq)), dma((shards, nq)),
            dma((shards + 1, nq)), dma((shards + 1, nq)),
            dma((parts,)), dma((parts,)),
            dma((shards,)), dma((shards,)),
            dma((shards,)), dma((shards,)),
            dma((shards,)), dma((shards,)),
            dma((maps, nq)), dma((maps, nq)),
            dma((3,)),
        ],
        compiler_params=pltpu.CompilerParams(
            collective_id=0, has_side_effects=True, vmem_limit_bytes=VMEM_BYTES
        ),
        name="features_project_scatter",
    )(tokens.reshape(tensors, sub, held), ffeat, ids, w_proj, probe, w_x, w_bc, wdt)
    return merged, proj.reshape(count, cols), dts, prb.reshape(count, wide), ids_out


def running(x, back):
    count = x.shape[1]
    lane = lax.broadcasted_iota(jnp.int32, x.shape, 1)
    k = 1
    while k < count:
        if back:
            x = x + jnp.where(lane < count - k, pltpu.roll(x, count - k, 1), 0.0)
        else:
            x = x + jnp.where(lane >= k, pltpu.roll(x, k, 1), 0.0)
        k *= 2
    return x


def mixer_kernel(proj, raw, prb, seg_row, seg_col, params, grads, gdt, grad_c, row):
    heads, count = raw.shape
    wide = prb.shape[1]
    tall = 128
    shifted = raw[...] + params[:, 0:1]
    dt = jnp.maximum(shifted, 0.0) + jnp.log1p(jnp.exp(-jnp.abs(shifted)))
    ld = running(-dt * params[:, 1:2], False)
    dt_cols, ld_cols = dt.T, ld.T
    grad_c[...] = jnp.zeros_like(grad_c)
    row[...] = jnp.zeros_like(row)
    cols = []
    for start in range(0, count, tall):
        at, after = slice(start, start + tall), slice(start, count)
        span = count - start
        b = proj[at, wide : wide + STATE]
        c = proj[after, wide + STATE :]
        nt = (((1,), (1,)), ((), ()))
        scores = lax.dot_general(b, c, nt, preferred_element_type=F32)
        lane = lax.broadcasted_iota(jnp.int32, (tall, span), 1)
        line = lax.broadcasted_iota(jnp.int32, (tall, span), 0)
        visible = (seg_col[at] == seg_row[:, after]) & (lane >= line)
        grad_s = jnp.zeros((tall, span), F32)
        col = []
        for h in range(heads):
            here = slice(h * HEAD_DIM, (h + 1) * HEAD_DIM)
            p = prb[after, here]
            step = dt_cols[at, h : h + 1]
            gap = ld[h : h + 1, after] - ld_cols[at, h : h + 1]
            decay = jnp.exp(jnp.where(visible, gap, -1e30))
            paired = decay * lax.dot_general(
                proj[at, here], p, nt, preferred_element_type=F32
            )
            grad_s = grad_s + paired * step
            mixed = (decay * scores).astype(BF16)
            grad_x = jnp.dot(mixed, p, preferred_element_type=F32) * step
            grad_x = grad_x + params[h : h + 1, 2:3] * prb[at, here].astype(F32)
            grads[at, here] = grad_x.astype(BF16)
            weighted = paired * scores
            col.append(jnp.sum(weighted, axis=1, keepdims=True))
            row[h : h + 1, after] += jnp.sum(weighted * step, axis=0, keepdims=True)
        grad_s = grad_s.astype(BF16)
        grads[at, wide : wide + STATE] = jnp.dot(
            grad_s, c, preferred_element_type=F32
        ).astype(BF16)
        grad_c[after] += lax.dot_general(
            grad_s, b, (((0,), (0,)), ((), ())), preferred_element_type=F32
        )
        cols.append(jnp.concatenate(col, axis=1))
    grads[:, wide + STATE :] = grad_c[...].astype(BF16)
    col = jnp.concatenate(cols, axis=0).T
    later = running(row[...] - col * dt, True)
    gdt[...] = (col - params[:, 1:2] * later) / (1.0 + jnp.exp(-shifted))


def mixer(proj, raw, prb, seg, params):
    count, cols = proj.shape
    heads = raw.shape[0]
    return pl.pallas_call(
        mixer_kernel,
        out_shape=(
            jax.ShapeDtypeStruct((count, cols), BF16),
            jax.ShapeDtypeStruct((heads, count), F32),
        ),
        in_specs=[pl.BlockSpec(memory_space=pltpu.VMEM)] * 6,
        out_specs=[pl.BlockSpec(memory_space=pltpu.VMEM)] * 2,
        scratch_shapes=[pltpu.VMEM((count, STATE), F32), pltpu.VMEM((heads, count), F32)],
        compiler_params=pltpu.CompilerParams(vmem_limit_bytes=VMEM_BYTES),
        name="mixer_gradient",
    )(proj, raw, prb, seg[None, :], seg[:, None], params)


def backward_kernel(
    shards, tensors, merged, grads, gdt, w_x_hbm, w_bc_hbm, wdt, step, frame_row, adv, frames,
    w_x, w_bc, every, out_bc, cross_bc, dt_all, acc, back, halves, home, mine, tile, tiles_t, tiles_p, picked, given,
    x_s, x_r, z_s, z_r, d_s, d_r, r_s, r_r, h_s, h_r, m_s, m_r, p_s, p_r, q_s, q_r, g_s, g_r, c_s, c_r, w_sem,
):
    parts = 2 * shards
    g, s, t = place()
    me = g * shards + s
    width = acc.shape[-1]
    sub = merged.shape[1]
    per = merged.shape[-1] // width
    count = shards * tensors * sub
    nq = grads.shape[0]
    span = shards // nq
    deep = tensors * sub

    def peer(i):
        p = lax.rem(me + i, parts)
        return p, (p // shards, lax.rem(p, shards), t)

    loads = [
        pltpu.make_async_copy(src, dst, w_sem.at[n])
        for n, (src, dst) in enumerate(((w_x_hbm, w_x), (w_bc_hbm, w_bc)))
    ]
    for load in loads:
        load.start()
    wide = w_x.shape[1] // shards
    pairs = shards // (w_bc.shape[1] // (2 * STATE))
    greet(parts, shards, tensors)

    def send_dt(i):
        p, device = peer(i)
        return rcopy(gdt, dt_all.at[me], d_s.at[i], d_r.at[i], device)

    def cross(j, q):
        at = every.at[g, j, q, :, :wide]
        return rcopy(at, at, x_s.at[j, q], x_r.at[j, q], (1 - g, s, t))

    def bc_cross(j, q):
        n = j // pairs
        return rcopy(out_bc.at[n, q], cross_bc.at[n, q], c_s.at[n, q], c_r.at[n, q], (1 - g, s, t))

    def right(j, q):
        return rcopy(every.at[g, j, q], every.at[g, j, q], z_s.at[0, j, q], z_r.at[j, q], (g, s + 1, t))

    def left(j, q):
        return rcopy(every.at[g, j, q], every.at[g, j, q], z_s.at[1, j, q], z_r.at[j, q], (g, s - 1, t))

    def each_way(j, q, what):
        @pl.when((j <= s) & (s < shards - 1))
        def _():
            what(right(j, q))

        @pl.when((j >= s) & (s > 0))
        def _():
            what(left(j, q))

        what(cross(j, q))

    for q in range(nq):
        every[g, s, q] = grads[q]
        each_way(s, q, lambda c: c.start())
    for i in range(1, parts):
        send_dt(i).start()
    dt_all[me] = gdt[...]
    for i in range(1, parts):
        q = lax.rem(me + parts - i, parts)
        p, device = peer(i)
        rcopy(gdt, dt_all.at[q], d_s.at[i], d_r.at[i], device).wait_recv()
    for gg in range(2):
        stack = jnp.concatenate([dt_all[gg * shards + k] for k in range(shards)], axis=0)
        acc[gg] = jnp.dot(
            stack.T.astype(BF16), wdt[...], preferred_element_type=F32
        ).reshape(nq, count // nq, width)

    nt = (((1,), (1,)), ((), ()))

    def add(gg, j, q):
        acc[gg, q] += lax.dot_general(
            every[gg, j, q, :, :wide], columns_of(w_x, j, wide), nt, preferred_element_type=F32
        )

    def add_bc(gg, j, q, ref):
        n = j // pairs
        acc[gg, q] += lax.dot_general(
            ref[n, q], columns_of(w_bc, n, 2 * STATE), nt, preferred_element_type=F32
        )

    def near(i):
        return far_first(shards - 1 - i, s, shards)

    def add_cross(i, q):
        j = near(i)
        at = every.at[1 - g, j, q, :, :wide]
        rcopy(at, at, x_s.at[j, q], x_r.at[j, q], (1 - g, s, t)).wait_recv()
        add(1 - g, j, q)
        if i % pairs == pairs - 1:
            bc_cross(j, q).wait_recv()
            add_bc(1 - g, j, q, cross_bc)

    for load in loads:
        load.wait()
    for q in range(nq):
        add(g, s, q)
    for i in range(1, shards):
        j = near(i)
        for q in range(nq):
            rcopy(
                every.at[g, j, q], every.at[g, j, q], x_s.at[j, q], z_r.at[j, q], (1 - g, s, t)
            ).wait_recv()
            each_way(j, q, lambda c: c.start())
            if i % pairs == pairs - 1:
                both = every[g, j, q, :, wide:].astype(F32)
                for n in range(1, pairs):
                    both = both + every[g, near(i - n), q, :, wide:].astype(F32)
                out_bc[j // pairs, q] = both.astype(BF16)
                bc_cross(j, q).start()
                add_bc(g, j, q, out_bc)
            add(g, j, q)
            add_cross(i - 1, q)

    steps = bits(tensors)

    def reduce_tensor(gg):
        for c in range(shards):
            q, k = c // span, c % span
            back[gg, c] = (
                acc[gg, q, k * deep : (k + 1) * deep].astype(BF16).reshape(tensors, sub, width)
            )
        low, size = 0, tensors
        for n, m in enumerate(steps):
            size //= 2
            bit = lax.rem(t // m, 2)
            keep, give = low + bit * size, low + (1 - bit) * size
            at = tensors - 2 * size
            copy = rcopy(
                back.at[gg, :, pl.ds(give, size)], halves.at[gg, :, pl.ds(at, size)],
                r_s.at[gg, n], r_r.at[gg, n], (g, s, t ^ m),
            )
            copy.start()
            copy.wait_recv()
            back[gg, :, pl.ds(keep, size)] = (
                back[gg, :, pl.ds(keep, size)].astype(F32)
                + halves[gg, :, at : at + size].astype(F32)
            ).astype(BF16)
            copy.wait_send()
            low = keep
        return low

    def send_home(gg, k):
        return rcopy(
            back.at[gg, k, spot], home.at[me], h_s.at[gg * shards + k], h_r.at[me], (gg, k, t)
        )

    def send_tile(gg, k):
        return rcopy(
            tile.at[gg], tiles_p.at[me], q_s.at[gg * shards + k], q_r.at[me], (gg, k, t)
        )

    def squares(gg):
        total = jnp.zeros((8, 128), F32)
        for k in range(shards):
            sq = back[gg, k, spot].astype(F32)
            sq = jnp.sum((sq * sq).reshape(sub // 8, 8, width), axis=0)
            for b in range(width // 128):
                total = total + sq[:, b * 128 : (b + 1) * 128]
        tile[gg] = total

    spot = reduce_tensor(g)
    for k in range(shards):
        @pl.when(k != s)
        def _():
            send_home(g, k).start()

    squares(g)
    for k in range(shards):
        @pl.when(k != s)
        def _():
            send_tile(g, k).start()

    home[me] = back[g, s, spot]
    tiles_p[me] = tile[g]
    for q in range(nq):
        add_cross(shards - 1, q)
    spot = reduce_tensor(1 - g)
    for k in range(shards):
        send_home(1 - g, k).start()
    squares(1 - g)
    for k in range(shards):
        send_tile(1 - g, k).start()
    for i in range(1, parts):
        p, device = peer(i)
        rcopy(home.at[p], home.at[p], h_s.at[p], h_r.at[p], device).wait_recv()

    def turn(m):
        at = pl.ds((t ^ m) * per, per)
        return rcopy(home.at[at], mine.at[spot], m_s.at[m], m_r.at[m], (g, s, t ^ m))

    def spot_of(tt):
        low, size = 0, tensors
        for m in steps:
            size //= 2
            low = low + lax.rem(tt // m, 2) * size
        return low

    for m in range(1, tensors):
        turn(m).start()
    mine[spot] = home[pl.ds(t * per, per)]
    for i in range(1, parts):
        p, device = peer(i)
        rcopy(tiles_p.at[p], tiles_p.at[p], q_s.at[p], q_r.at[p], device).wait_recv()
    total = tiles_p[0]
    for p in range(1, parts):
        total = total + tiles_p[p]
    tile[2] = total

    def share_t(m):
        return rcopy(tile.at[2], tiles_t.at[m], p_s.at[m], p_r.at[m], (g, s, t ^ m))

    for m in range(1, tensors):
        share_t(m).start()
    for m in range(1, tensors):
        at = spot_of(t ^ m)
        rcopy(mine.at[at], mine.at[at], m_s.at[m], m_r.at[m], (g, s, t ^ m)).wait_recv()
    for m in range(1, tensors):
        share_t(m).wait_recv()
        total = total + tiles_t[m]
    entries = count * parts * width
    scale = lax.rsqrt(jnp.sum(total, keepdims=True) / entries + 1e-06)
    for n in range(tensors):
        move = step[n] * scale
        for h in range(per):
            at = slice(h * width, (h + 1) * width)
            adv[n, :, at] = (
                merged[n, :, at].astype(F32) + move * mine[n, h].astype(F32)
            ).astype(BF16)

    slots = picked.shape[1]
    hot = one_hot(frame_row[0:1], s, deep).T[: shards * slots].astype(BF16)
    chosen = jnp.dot(hot, adv[...].reshape(deep, -1), preferred_element_type=F32)
    picked[...] = chosen.astype(BF16).reshape(picked.shape)

    def give_back(i):
        k = lax.rem(s + i, shards)
        return rcopy(picked.at[k], given.at[i], g_s.at[i], g_r.at[i], (g, k, t))

    for i in range(1, shards):
        give_back(i).start()
    total = picked[s].astype(F32)
    for i in range(1, shards):
        give_back(i).wait_recv()
        total = total + given[i].astype(F32)
    frames[...] = total.astype(BF16)

    for i in range(1, parts):
        send_dt(i).wait_send()
    for m in range(1, tensors):
        turn(m).wait_send()
        share_t(m).wait_send()
    for i in range(1, shards):
        give_back(i).wait_send()
    for k in range(shards):
        @pl.when(k != s)
        def _():
            send_home(g, k).wait_send()
            send_tile(g, k).wait_send()

        send_home(1 - g, k).wait_send()
        send_tile(1 - g, k).wait_send()

    def end(j, carry):
        for q in range(nq):
            @pl.when(lax.rem(j, pairs) == 0)
            def _():
                bc_cross(j, q).wait_send()

            each_way(j, q, lambda c: c.wait_send())
        return carry

    lax.fori_loop(0, shards, end, 0)


def backward(merged, grads, gdt, w_x, w_bc, wdt, direction, frame_row, slots, shards):
    parts = 2 * shards
    tensors, sub, held = merged.shape
    rows = tensors * sub
    width = w_x.shape[0]
    cols = grads.shape[1]
    count = rows * shards
    per = held // width
    heads = gdt.shape[0]
    nq = 2
    maps = w_bc.shape[1] // (2 * STATE)
    block = (count // nq, cols)
    dma = pltpu.SemaphoreType.DMA
    levels = len(bits(tensors))
    adv, frames = pl.pallas_call(
        functools.partial(backward_kernel, shards, tensors),
        out_shape=(
            jax.ShapeDtypeStruct((tensors, sub, held), BF16),
            jax.ShapeDtypeStruct((slots, held), BF16),
        ),
        in_specs=[
            pl.BlockSpec(memory_space=pl.ANY if n in (3, 4) else pltpu.VMEM) for n in range(8)
        ],
        out_specs=[pl.BlockSpec(memory_space=pltpu.VMEM)] * 2,
        scratch_shapes=[
            pltpu.VMEM(w_x.shape, BF16),
            pltpu.VMEM(w_bc.shape, BF16),
            pltpu.VMEM((2, shards, nq) + block, BF16),
            pltpu.VMEM((maps, nq, count // nq, 2 * STATE), BF16),
            pltpu.VMEM((maps, nq, count // nq, 2 * STATE), BF16),
            pltpu.VMEM((parts, heads, count), F32),
            pltpu.VMEM((2, nq, count // nq, width), F32),
            pltpu.VMEM((2, shards, tensors, sub, width), BF16),
            pltpu.VMEM((2, shards, tensors, sub, width), BF16),
            pltpu.VMEM((parts, sub, width), BF16),
            pltpu.VMEM((tensors, per, sub, width), BF16),
            pltpu.VMEM((3, 8, 128), F32),
            pltpu.VMEM((tensors, 8, 128), F32),
            pltpu.VMEM((parts, 8, 128), F32),
            pltpu.VMEM((shards, slots, held), BF16),
            pltpu.VMEM((shards, slots, held), BF16),
            dma((shards, nq)), dma((shards, nq)),
            dma((2, shards, nq)), dma((shards, nq)),
            dma((parts,)), dma((parts,)),
            dma((2, levels)), dma((2, levels)),
            dma((parts,)), dma((parts,)),
            dma((tensors,)), dma((tensors,)),
            dma((tensors,)), dma((tensors,)),
            dma((parts,)), dma((parts,)),
            dma((shards,)), dma((shards,)),
            dma((maps, nq)), dma((maps, nq)),
            dma((2,)),
        ],
        compiler_params=pltpu.CompilerParams(
            collective_id=1, has_side_effects=True, vmem_limit_bytes=VMEM_BYTES
        ),
        name="gather_project_step",
    )(
        merged,
        grads.reshape((nq,) + block),
        gdt,
        w_x,
        w_bc,
        wdt,
        direction.reshape(tensors, sub, 1),
        frame_row,
    )
    return adv.reshape(rows, held), frames


def in_vmem(groups, shards, tensors, rows, width, cols, slots, pairs):
    if groups != 2 or shards % 2 or tensors & (tensors - 1) or rows % (16 * tensors):
        return False
    if rows != 128 or slots * shards > 128 or shards != 4 or pairs not in (1, 2):
        return False
    if width % 128 or cols % 128 or shards * width * 2 % tensors:
        return False
    count = rows * shards
    lines = 2 * count * cols * (4 * shards + 1)
    sums = 2 * count * width * 4 + 4 * count * cols * shards
    return max(lines, sums) + 2 * width * cols * shards + 8 * count * width < VMEM_BYTES // 2


def mixer_grad(x, b, c, pdt, probe, seg, dt_bias, decay_rate, skip_gain):
    count, heads = pdt.shape
    shifted = pdt + dt_bias[None, :]
    dt = jax.nn.softplus(shifted).T
    ld = jnp.cumsum(-dt * decay_rate[:, None], axis=1)
    position = jnp.arange(count)
    visible = (seg[:, None] == seg[None, :]) & (position[:, None] >= position[None, :])
    gap = ld[:, :, None] - ld[:, None, :]
    decay = jnp.where(visible[None], jnp.exp(jnp.where(visible[None], gap, 0.0)), 0.0)
    xh = x.astype(BF16).reshape(count, heads, HEAD_DIM)
    ph = probe.reshape(count, heads, HEAD_DIM)
    bb, cb = b.astype(BF16), c.astype(BF16)
    scores = jnp.dot(cb, bb.T, preferred_element_type=F32)
    pairs = jnp.einsum("thp,shp->hts", ph, xh, preferred_element_type=F32)
    mixed = decay * scores[None]
    grad_x = jnp.einsum("hts,thp->shp", mixed.astype(BF16), ph, preferred_element_type=F32)
    grad_x = grad_x * dt.T[:, :, None] + skip_gain[None, :, None] * ph.astype(F32)
    weighted = mixed * pairs
    col = jnp.sum(weighted, axis=1)
    row = jnp.sum(weighted * dt[:, None, :], axis=2)
    grad_s = jnp.sum(decay * pairs * dt[:, None, :], axis=0).astype(BF16)
    grad_c = jnp.dot(grad_s, bb, preferred_element_type=F32)
    grad_b = jnp.dot(grad_s.T, cb, preferred_element_type=F32)
    grad_ld = row - col * dt
    later = jnp.cumsum(grad_ld[:, ::-1], axis=1)[:, ::-1]
    grad_dt = (col - decay_rate[:, None] * later).T * jax.nn.sigmoid(shifted)
    return grad_x.reshape(count, -1), grad_b, grad_c, grad_dt


def by_collectives(
    tokens,
    frame_feats,
    w_proj,
    frame_pos,
    segments,
    signs,
    w_x,
    w_bc,
    w_dt,
    dt_bias,
    decay_rate,
    skip_gain,
    probe,
):
    rows = tokens.shape[1]
    groups, shards, tensors = (lax.axis_size(a) for a in ("group", "seq", "tensor"))
    g, s, t = (lax.axis_index(a) for a in ("group", "seq", "tensor"))
    parts = groups * shards
    count = rows * shards
    width = w_x.shape[0]
    heads = w_dt.shape[1] // shards
    per_group = w_dt.shape[1] * 2 * STATE // w_bc.shape[1]
    cols_x = heads * HEAD_DIM
    group_of = [(k * heads) // per_group for k in range(shards)]
    cols = cols_x + 2 * STATE + heads

    feats, pos = (
        lax.all_to_all(frame_feats[0], "seq", split_axis=0, concat_axis=0, tiled=True),
        lax.all_to_all(frame_pos[0], "seq", split_axis=0, concat_axis=0, tiled=True),
    )
    local_pos = pos - s * rows
    arrived = jnp.dot(feats, w_proj, preferred_element_type=F32).astype(BF16)
    merged = tokens[0].at[local_pos].set(arrived)

    sub = rows // tensors
    f = lax.all_to_all(merged, "tensor", split_axis=0, concat_axis=1, tiled=True)
    f = f.reshape(sub, parts, width).transpose(1, 0, 2)
    f = lax.all_to_all(f, ("group", "seq"), split_axis=0, concat_axis=0, tiled=True)
    f = lax.all_gather(f, "tensor", axis=1, tiled=True)
    f = f.reshape(groups, count, width)

    weights = jnp.stack(
        [
            jnp.concatenate(
                [
                    w_x[:, k * cols_x : (k + 1) * cols_x],
                    w_bc[:, group_of[k] * 2 * STATE : (group_of[k] + 1) * 2 * STATE],
                    w_dt[:, k * heads : (k + 1) * heads],
                ],
                axis=1,
            )
            for k in range(shards)
        ]
    )
    partial = jnp.einsum("gtk,skc->gstc", f, weights, preferred_element_type=F32).astype(BF16)
    proj = lax.psum_scatter(
        partial.reshape(parts, count, cols), ("group", "seq"), scatter_dimension=0, tiled=False
    ).astype(F32)

    seg = lax.all_gather(segments[0], "seq", axis=0, tiled=True)
    prb = lax.all_to_all(
        probe[0].reshape(rows, shards, cols_x).transpose(1, 0, 2),
        "seq",
        split_axis=0,
        concat_axis=0,
        tiled=True,
    ).reshape(count, cols_x)

    def own(v):
        return lax.dynamic_slice(v, (s * heads,), (heads,))

    grads = mixer_grad(
        proj[:, :cols_x],
        proj[:, cols_x : cols_x + STATE],
        proj[:, cols_x + STATE : cols_x + 2 * STATE],
        proj[:, cols_x + 2 * STATE :],
        prb,
        seg,
        own(dt_bias),
        own(decay_rate),
        own(skip_gain),
    )
    grads = jnp.concatenate([v.astype(BF16) for v in grads], axis=1)
    every = lax.all_gather(grads, ("group", "seq"), axis=0, tiled=False)
    every = every.reshape(groups, shards, count, cols)
    back = jnp.einsum("gstc,skc->gtk", every, weights, preferred_element_type=F32).astype(BF16)

    back = back.reshape(parts, tensors, sub, width).transpose(1, 0, 2, 3)
    back = lax.all_to_all(back, "tensor", split_axis=0, concat_axis=0, tiled=True)
    summed = jnp.sum(back.astype(F32), axis=0)
    squares = jnp.sum(summed.reshape(groups, -1) ** 2, axis=1)
    squares = lax.psum(squares, ("group", "seq", "tensor"))[g]
    home = lax.all_to_all(
        summed.astype(BF16), ("group", "seq"), split_axis=0, concat_axis=0, tiled=True
    )
    home = home.transpose(1, 0, 2).reshape(sub, tensors, -1).transpose(1, 0, 2)
    gradient = lax.all_to_all(home, "tensor", split_axis=0, concat_axis=0, tiled=True)
    gradient = gradient.reshape(rows, -1).astype(F32)

    entries = count * parts * width
    grad_scale = jnp.sqrt(squares / entries + 1e-06)
    direction = (2 * signs[0] - 1).astype(F32)[:, None]
    adv = (merged.astype(F32) + 0.5 * direction * gradient / grad_scale).astype(BF16)
    picked = adv[local_pos]
    returned = lax.all_to_all(picked, "seq", split_axis=0, concat_axis=0, tiled=True)
    return (adv[None], returned[None])


def body(*arrays):
    tokens, frame_feats, w_x, w_dt = arrays[0], arrays[1], arrays[6], arrays[8]
    sizes = tuple(lax.axis_size(a) for a in ("group", "seq", "tensor"))
    cols = w_dt.shape[1] // sizes[1] * HEAD_DIM + 2 * STATE
    slots = -(-frame_feats.shape[1] // 16) * 16
    pairs = sizes[1] * 2 * STATE // arrays[7].shape[1]
    if in_vmem(*sizes, tokens.shape[1], w_x.shape[0], cols, slots, pairs):
        return by_kernels(slots, *arrays)
    return by_collectives(*arrays)


def by_kernels(
    slots,
    tokens,
    frame_feats,
    w_proj,
    frame_pos,
    segments,
    signs,
    w_x,
    w_bc,
    w_dt,
    dt_bias,
    decay_rate,
    skip_gain,
    probe,
):
    shards, tensors = lax.axis_size("seq"), lax.axis_size("tensor")
    s = lax.axis_index("seq")
    frames = frame_feats.shape[1]
    heads = w_dt.shape[1] // shards
    ffeat = jnp.pad(frame_feats[0], ((0, slots - frames), (0, 0)))
    lane = jnp.full((shards, slots), -1, jnp.int32)
    lane = lax.dynamic_update_slice(lane, frame_pos, (s, 0)).reshape(1, -1)
    lane = jnp.pad(lane, ((0, 0), (0, 128 - shards * slots)), constant_values=-1)
    ids = jnp.concatenate([jnp.broadcast_to(v, (8, 128)) for v in (lane, segments)], axis=0)
    w_step = w_dt.T
    merged, proj, raw, prb, ids = forward(
        tokens[0], ffeat, ids, w_proj, probe[0], w_x, w_bc, w_step, shards, tensors, heads
    )
    params = jnp.stack([dt_bias, decay_rate, skip_gain], axis=1)
    params = lax.dynamic_slice(params, (s * heads, 0), (heads, 3))
    grads, gdt = mixer(proj, raw, prb, ids[1:, 0].reshape(-1), params)
    direction = 0.5 * (2 * signs[0] - 1).astype(F32)
    adv, returned = backward(
        merged, grads, gdt, w_x, w_bc, w_step, direction, ids[0], slots, shards
    )
    return (adv[None], returned[None, :frames])


def solution(mesh):
    return jax.shard_map(
        body,
        mesh=mesh,
        in_specs=(
            P("group", "seq", "tensor"),
            P("group", "seq", None),
            P(None, "tensor"),
            P("group", "seq"),
            P("group", "seq"),
            P("group", "seq"),
            P(("group", "seq"), "tensor"),
            P(("group", "seq"), "tensor"),
            P(("group", "seq"), "tensor"),
            P("tensor"),
            P("tensor"),
            P("tensor"),
            P("group", "seq", "tensor"),
        ),
        out_specs=(P("group", "seq", "tensor"), P("group", "seq", "tensor")),
        check_vma=False,
    )
```

```python
import functools

import jax
import jax.numpy as jnp
from jax import lax
from jax.experimental import pallas as pl
from jax.experimental.pallas import tpu as pltpu
from jax.sharding import PartitionSpec as P

HEAD_DIM = 64
STATE = 128
BF16 = jnp.bfloat16
F32 = jnp.float32


MESH = pl.DeviceIdType.MESH
VMEM_BYTES = 58 * 2**20


def place():
    return tuple(lax.axis_index(a) for a in ("group", "seq", "tensor"))


def rcopy(src, dst, send, recv, device):
    return pltpu.make_async_remote_copy(
        src_ref=src, dst_ref=dst, send_sem=send, recv_sem=recv, device_id=device, device_id_type=MESH
    )


def far_first(i, s, shards):
    down = jnp.where(i < shards - 1 - s, shards - 1 - i, shards - 2 - i)
    up = jnp.where(i < s, i, i + 1)
    other = jnp.where(2 * s < shards, down, up)
    return jnp.where(i == shards - 1, s, other)


def greet(parts, shards, tensors, per):
    g, s, t = place()
    me = g * shards + s
    barrier = pltpu.get_barrier_semaphore()
    for i in range(1, parts):
        p = lax.rem(me + i, parts)
        pl.semaphore_signal(
            barrier, inc=1, device_id=(p // shards, lax.rem(p, shards), t), device_id_type=MESH
        )
    for m in range(1, tensors):
        pl.semaphore_signal(barrier, inc=1, device_id=(g, s, t ^ m), device_id_type=MESH)

    def hello(p, tt):
        pl.semaphore_signal(
            barrier, inc=1, device_id=(p // shards, lax.rem(p, shards), tt), device_id_type=MESH
        )

    for p in range(parts):
        hello(p, me // per)
    for h in range(per):
        for m in range(tensors):
            hello(t * per + h, t ^ m)
    pl.semaphore_wait(barrier, parts + tensors - 2 + parts + per * tensors)


def bits(tensors):
    m, out = 1, []
    while m < tensors:
        out.append(m)
        m *= 2
    return out


def columns_of(w, k, wide):
    return w[:, pl.ds(pl.multiple_of(k * wide, 128), wide)]


def one_hot(frame_row, s, rows):
    position = lax.broadcasted_iota(jnp.int32, (rows, 128), 0) + s * rows
    return jnp.where(position == frame_row, 1.0, 0.0).astype(F32)


def forward_kernel(
    shards, tensors, heads, tokens, ffeat, ids, w_proj_hbm, probe, w_x_hbm, w_bc_hbm, wdt,
    merged, proj, dts, prb, ids_out,
    w_proj, w_x, w_bc, feats, outgo, cross, out_bc, cross_bc, own, line, dt_part, dt_all, ff_all, ids_all, prb_all,
    f_s, f_r, h_s, h_r, x_s, x_r, z_s, z_r, d_s, d_r, e_s, e_r, i_s, i_r, b_s, b_r, c_s, c_r, w_sem,
):
    parts = 2 * shards
    g, s, t = place()
    me = g * shards + s
    width = feats.shape[-1]
    sub = feats.shape[2]
    per = merged.shape[-1] // width
    count = shards * tensors * sub
    nq = proj.shape[0]
    span = shards // nq

    def peer(i):
        p = lax.rem(me + i, parts)
        return p, (p // shards, lax.rem(p, shards), t)

    loads = [
        pltpu.make_async_copy(src, dst, w_sem.at[n])
        for n, (src, dst) in enumerate(((w_proj_hbm, w_proj), (w_x_hbm, w_x), (w_bc_hbm, w_bc)))
    ]
    for load in loads:
        load.start()
    wide = w_x.shape[1] // shards
    pairs = shards // (w_bc.shape[1] // (2 * STATE))
    greet(parts, shards, tensors, per)

    def seq_peer(i):
        return (g, lax.rem(s + i, shards), t)

    def send_ids(i):
        return rcopy(ids, ids_all.at[s], i_s.at[i], i_r.at[i], seq_peer(i))

    def send_ff(i):
        return rcopy(ffeat, ff_all.at[s], e_s.at[i], e_r.at[i], seq_peer(i))

    def send_probe(i):
        k = lax.rem(s + i, shards)
        wide = probe.shape[1] // shards
        at = pl.ds(pl.multiple_of(k * wide, 128), wide)
        return rcopy(probe.at[:, at], prb_all.at[s], b_s.at[i], b_r.at[i], seq_peer(i))

    for i in range(1, shards):
        send_ids(i).start()
        send_ff(i).start()
    ids_all[s] = ids[...]
    ff_all[s] = ffeat[...]
    for i in range(1, shards):
        k = lax.rem(s + shards - i, shards)
        rcopy(ids, ids_all.at[k], i_s.at[i], i_r.at[i], seq_peer(i)).wait_recv()
        rcopy(ffeat, ff_all.at[k], e_s.at[i], e_r.at[i], seq_peer(i)).wait_recv()
    frame_row = ids_all[0, 0:8]
    for k in range(1, shards):
        frame_row = jnp.maximum(frame_row, ids_all[k, 0:8])
    ids_out[0] = frame_row
    for k in range(shards):
        ids_out[1 + k] = ids_all[k, 8:16]
    slots = shards * ffeat.shape[0]
    loads[0].wait()
    emb = jnp.dot(
        ff_all[...].reshape(slots, ffeat.shape[1]), w_proj[...], preferred_element_type=F32
    ).astype(BF16)
    hot = one_hot(frame_row[0:1], s, tensors * sub)
    taken = jnp.sum(hot, axis=1, keepdims=True)
    placed = jnp.dot(hot[:, :slots].astype(BF16), emb, preferred_element_type=F32)
    for n in range(tensors):
        at = slice(n * sub, (n + 1) * sub)
        merged[n] = jnp.where(taken[at] > 0.5, placed[at], tokens[n].astype(F32)).astype(BF16)

    def columns(h):
        return slice(h * width, (h + 1) * width)

    def spread(h, m):
        r = t * per + h
        return rcopy(
            merged.at[t ^ m, :, columns(h)], feats.at[me, t ^ m], f_s.at[h, m], f_r.at[me],
            (r // shards, lax.rem(r, shards), t ^ m),
        )

    def spread_all(what):
        for h in range(per):
            for m in range(1, tensors):
                what(spread(h, m))

            @pl.when(t * per + h != me)
            def _():
                what(spread(h, 0))

    spread_all(lambda c: c.start())
    for h in range(per):
        @pl.when(t * per + h == me)
        def _():
            feats[me, t] = merged[t, :, columns(h)]

    def arrived(gg):
        for k in range(shards):
            p = gg * shards + k
            holder = me // per

            @pl.when((p != me) | (holder != t))
            def _():
                rcopy(
                    feats.at[p, t], feats.at[p, t], f_s.at[0, 0], f_r.at[p], (1 - g, s, t)
                ).wait_recv()

    arrived(1 - g)

    def pass_on(gg, m, c, n):
        at = feats.at[pl.ds(gg * shards, shards), t ^ c]
        return rcopy(at, at, h_s.at[n, m | c], h_r.at[n, m | c], (g, s, t ^ m))

    def over_tensor(gg, n):
        held = [0]
        for m in reversed(bits(tensors)):
            for c in held:
                pass_on(gg, m, c, n).start()
            for c in held:
                at = feats.at[pl.ds(gg * shards, shards), t ^ (m | c)]
                rcopy(at, at, h_s.at[n, m | c], h_r.at[n, m | c], (g, s, t ^ m)).wait_recv()
            held = held + [m | c for c in held]

    over_tensor(1 - g, 0)

    def product(gg, q, w):
        rows = feats[pl.ds(gg * shards + q * span, span)].reshape(count // nq, width)
        return jnp.dot(rows, w, preferred_element_type=F32).astype(BF16)

    def for_x(gg, d, q):
        return product(gg, q, columns_of(w_x, d, wide))

    def for_bc(gg, d, q):
        return product(gg, q, columns_of(w_bc, d // pairs, 2 * STATE))

    def to_cross(d, q):
        return rcopy(outgo.at[d, q], cross.at[d, q], x_s.at[d, q], x_r.at[d, q], (1 - g, s, t))

    def bc_to_cross(d, q):
        n = d // pairs
        return rcopy(out_bc.at[n, q], cross_bc.at[n, q], c_s.at[n, q], c_r.at[n, q], (1 - g, s, t))

    loads[1].wait()
    loads[2].wait()

    def first(i, carry):
        d = far_first(i, s, shards)
        for q in range(nq):
            outgo[d, q] = for_x(1 - g, d, q)
            to_cross(d, q).start()

            @pl.when(lax.rem(i, pairs) == 0)
            def _():
                out_bc[d // pairs, q] = for_bc(1 - g, d, q)
                bc_to_cross(d, q).start()

        return carry

    lax.fori_loop(0, shards, first, 0)
    for i in range(1, shards):
        send_probe(i).start()
    prb_all[s] = probe[:, pl.ds(pl.multiple_of(s * wide, 128), wide)]
    arrived(g)
    over_tensor(g, 1)

    for gg in range(2):
        rows = feats[gg * shards : (gg + 1) * shards].reshape(count, width)
        steps = lax.dot_general(
            wdt[...], rows, (((1,), (1,)), ((), ())), preferred_element_type=F32
        )
        for k in range(shards):
            dt_part[gg * shards + k] = steps[k * heads : (k + 1) * heads]

    def send_dt(i):
        p, device = peer(i)
        return rcopy(dt_part.at[p], dt_all.at[me], d_s.at[i], d_r.at[i], device)

    for i in range(1, parts):
        send_dt(i).start()
    dt_all[me] = dt_part[me]

    def right(d, q):
        return rcopy(own.at[d, q], line.at[d, q], z_s.at[d, q], z_r.at[d, q], (g, s + 1, t))

    def left(d, q):
        slot = jnp.where(d == s - 1, shards, d)
        return rcopy(own.at[d, q], line.at[slot, q], z_s.at[d, q], z_r.at[slot, q], (g, s - 1, t))

    def come(slot, q):
        rcopy(
            line.at[slot, q], line.at[slot, q], z_s.at[slot, q], z_r.at[slot, q], (1 - g, s, t)
        ).wait_recv()

    def both_samples(d, q):
        mine_x = own[d, q, :, :wide].astype(F32) + cross[d, q].astype(F32)
        mine_bc = own[d, q, :, wide:].astype(F32) + cross_bc[d // pairs, q].astype(F32)
        return jnp.concatenate([mine_x, mine_bc], axis=1)

    def second(i, carry):
        d = far_first(i, s, shards)
        for q in range(nq):
            own[d, q, :, :wide] = for_x(g, d, q)
            own[d, q, :, wide:] = for_bc(g, d, q)
        for q in range(nq):
            to_cross(d, q).wait_recv()

            @pl.when(lax.rem(i, pairs) == 0)
            def _():
                bc_to_cross(d, q).wait_recv()

            has_more = ((d > s) & (s > 0)) | ((d < s) & (s < shards - 1))

            @pl.when(has_more)
            def _():
                come(d, q)
                own[d, q] = (both_samples(d, q) + line[d, q].astype(F32)).astype(BF16)

            @pl.when(jnp.logical_not(has_more))
            def _():
                own[d, q] = both_samples(d, q).astype(BF16)

            @pl.when(d > s)
            def _():
                right(d, q).start()

            @pl.when(d < s)
            def _():
                left(d, q).start()

        return carry

    lax.fori_loop(0, shards - 1, second, 0)
    for q in range(nq):
        own[s, q, :, :wide] = for_x(g, s, q)
        own[s, q, :, wide:] = for_bc(g, s, q)
    for q in range(nq):
        to_cross(s, q).wait_recv()
        own[s, q] = both_samples(s, q).astype(BF16)

        @pl.when(s > 0)
        def _():
            come(s, q)
            own[s, q] = (own[s, q].astype(F32) + line[s, q].astype(F32)).astype(BF16)

        @pl.when(s < shards - 1)
        def _():
            come(shards, q)
            own[s, q] = (own[s, q].astype(F32) + line[shards, q].astype(F32)).astype(BF16)

        proj[q] = own[s, q]

    for i in range(1, parts):
        q = lax.rem(me + parts - i, parts)
        p, device = peer(i)
        rcopy(dt_part.at[p], dt_all.at[q], d_s.at[i], d_r.at[i], device).wait_recv()
    total = dt_all[0]
    for p in range(1, parts):
        total = total + dt_all[p]
    dts[...] = total

    for i in range(1, shards):
        k = lax.rem(s + shards - i, shards)
        rcopy(prb_all.at[k], prb_all.at[k], b_s.at[i], b_r.at[i], seq_peer(i)).wait_recv()
    prb[...] = prb_all[...]

    for i in range(1, shards):
        send_ids(i).wait_send()
        send_ff(i).wait_send()
        send_probe(i).wait_send()
    spread_all(lambda c: c.wait_send())
    for i in range(1, parts):
        send_dt(i).wait_send()
    for n, gg in enumerate((1 - g, g)):
        held = [0]
        for m in reversed(bits(tensors)):
            for c in held:
                pass_on(gg, m, c, n).wait_send()
            held = held + [m | c for c in held]

    def last(d, carry):
        for q in range(nq):
            to_cross(d, q).wait_send()

            @pl.when(lax.rem(d, pairs) == 0)
            def _():
                bc_to_cross(d, q).wait_send()

            @pl.when(d > s)
            def _():
                right(d, q).wait_send()

            @pl.when(d < s)
            def _():
                left(d, q).wait_send()

        return carry

    lax.fori_loop(0, shards, last, 0)


def forward(tokens, ffeat, ids, w_proj, probe, w_x, w_bc, wdt, shards, tensors, heads):
    parts = 2 * shards
    rows, held = tokens.shape
    sub = rows // tensors
    width = w_x.shape[0]
    wide = w_x.shape[1] // shards
    maps = w_bc.shape[1] // (2 * STATE)
    cols = wide + 2 * STATE
    count = rows * shards
    nq = 2
    block = (count // nq, cols)
    dma = pltpu.SemaphoreType.DMA
    merged, proj, dts, prb, ids_out = pl.pallas_call(
        functools.partial(forward_kernel, shards, tensors, heads),
        out_shape=(
            jax.ShapeDtypeStruct((tensors, sub, held), BF16),
            jax.ShapeDtypeStruct((nq,) + block, BF16),
            jax.ShapeDtypeStruct((heads, count), F32),
            jax.ShapeDtypeStruct((shards, rows, wide), BF16),
            jax.ShapeDtypeStruct((1 + shards, 8, 128), jnp.int32),
        ),
        in_specs=[
            pl.BlockSpec(memory_space=pl.ANY if n in (3, 5, 6) else pltpu.VMEM) for n in range(8)
        ],
        out_specs=[pl.BlockSpec(memory_space=pltpu.VMEM)] * 5,
        scratch_shapes=[
            pltpu.VMEM(w_proj.shape, BF16),
            pltpu.VMEM(w_x.shape, BF16),
            pltpu.VMEM(w_bc.shape, BF16),
            pltpu.VMEM((parts, tensors, sub, width), BF16),
            pltpu.VMEM((shards, nq, count // nq, wide), BF16),
            pltpu.VMEM((shards, nq, count // nq, wide), BF16),
            pltpu.VMEM((maps, nq, count // nq, 2 * STATE), BF16),
            pltpu.VMEM((maps, nq, count // nq, 2 * STATE), BF16),
            pltpu.VMEM((shards, nq) + block, BF16),
            pltpu.VMEM((shards + 1, nq) + block, BF16),
            pltpu.VMEM((parts, heads, count), F32),
            pltpu.VMEM((parts, heads, count), F32),
            pltpu.VMEM((shards,) + ffeat.shape, BF16),
            pltpu.VMEM((shards,) + ids.shape, jnp.int32),
            pltpu.VMEM((shards, rows, wide), BF16),
            dma((held // width, tensors)), dma((parts,)),
            dma((2, tensors)), dma((2, tensors)),
            dma((shards, nq)), dma((shards, nq)),
            dma((shards + 1, nq)), dma((shards + 1, nq)),
            dma((parts,)), dma((parts,)),
            dma((shards,)), dma((shards,)),
            dma((shards,)), dma((shards,)),
            dma((shards,)), dma((shards,)),
            dma((maps, nq)), dma((maps, nq)),
            dma((3,)),
        ],
        compiler_params=pltpu.CompilerParams(
            collective_id=0, has_side_effects=True, vmem_limit_bytes=VMEM_BYTES
        ),
        name="features_project_scatter",
    )(tokens.reshape(tensors, sub, held), ffeat, ids, w_proj, probe, w_x, w_bc, wdt)
    return merged, proj.reshape(count, cols), dts, prb.reshape(count, wide), ids_out


def running(x, back):
    count = x.shape[1]
    lane = lax.broadcasted_iota(jnp.int32, x.shape, 1)
    k = 1
    while k < count:
        if back:
            x = x + jnp.where(lane < count - k, pltpu.roll(x, count - k, 1), 0.0)
        else:
            x = x + jnp.where(lane >= k, pltpu.roll(x, k, 1), 0.0)
        k *= 2
    return x


def mixer_kernel(proj, raw, prb, ids, params, grads, gdt, grad_c, row):
    heads, count = raw.shape
    wide = prb.shape[1]
    tall = 128
    shifted = raw[...] + params[:, 0:1]
    dt = jnp.maximum(shifted, 0.0) + jnp.log1p(jnp.exp(-jnp.abs(shifted)))
    ld = running(-dt * params[:, 1:2], False)
    dt_cols, ld_cols = dt.T, ld.T
    segs = [ids[k].astype(F32) for k in range(1, ids.shape[0])]
    seg_row = jnp.concatenate([v[0:1] for v in segs], axis=1)
    seg_col = [v.T[:, 0:1] for v in segs]
    grad_c[...] = jnp.zeros_like(grad_c)
    row[...] = jnp.zeros_like(row)
    cols = []
    for start in range(0, count, tall):
        at, after = slice(start, start + tall), slice(start, count)
        span = count - start
        b = proj[at, wide : wide + STATE]
        c = proj[after, wide + STATE :]
        nt = (((1,), (1,)), ((), ()))
        scores = lax.dot_general(b, c, nt, preferred_element_type=F32)
        lane = lax.broadcasted_iota(jnp.int32, (tall, span), 1)
        line = lax.broadcasted_iota(jnp.int32, (tall, span), 0)
        visible = (seg_col[start // tall] == seg_row[:, after]) & (lane >= line)
        grad_s = jnp.zeros((tall, span), F32)
        col = []
        for h in range(heads):
            here = slice(h * HEAD_DIM, (h + 1) * HEAD_DIM)
            p = prb[after, here]
            step = dt_cols[at, h : h + 1]
            gap = ld[h : h + 1, after] - ld_cols[at, h : h + 1]
            decay = jnp.exp(jnp.where(visible, gap, -1e30))
            paired = decay * lax.dot_general(
                proj[at, here], p, nt, preferred_element_type=F32
            )
            grad_s = grad_s + paired * step
            mixed = (decay * scores).astype(BF16)
            grad_x = jnp.dot(mixed, p, preferred_element_type=F32) * step
            grad_x = grad_x + params[h : h + 1, 2:3] * prb[at, here].astype(F32)
            grads[at, here] = grad_x.astype(BF16)
            weighted = paired * scores
            col.append(jnp.sum(weighted, axis=1, keepdims=True))
            row[h : h + 1, after] += jnp.sum(weighted * step, axis=0, keepdims=True)
        grad_s = grad_s.astype(BF16)
        grads[at, wide : wide + STATE] = jnp.dot(
            grad_s, c, preferred_element_type=F32
        ).astype(BF16)
        grad_c[after] += lax.dot_general(
            grad_s, b, (((0,), (0,)), ((), ())), preferred_element_type=F32
        )
        cols.append(jnp.concatenate(col, axis=1))
    grads[:, wide + STATE :] = grad_c[...].astype(BF16)
    col = jnp.concatenate(cols, axis=0).T
    later = running(row[...] - col * dt, True)
    gdt[...] = (col - params[:, 1:2] * later) / (1.0 + jnp.exp(-shifted))


def mixer(proj, raw, prb, ids, params):
    count, cols = proj.shape
    heads = raw.shape[0]
    return pl.pallas_call(
        mixer_kernel,
        out_shape=(
            jax.ShapeDtypeStruct((count, cols), BF16),
            jax.ShapeDtypeStruct((heads, count), F32),
        ),
        in_specs=[pl.BlockSpec(memory_space=pltpu.VMEM)] * 5,
        out_specs=[pl.BlockSpec(memory_space=pltpu.VMEM)] * 2,
        scratch_shapes=[pltpu.VMEM((count, STATE), F32), pltpu.VMEM((heads, count), F32)],
        compiler_params=pltpu.CompilerParams(vmem_limit_bytes=VMEM_BYTES),
        name="mixer_gradient",
    )(proj, raw, prb, ids, params)


def backward_kernel(
    shards, tensors, merged, grads, gdt, w_x_hbm, w_bc_hbm, wdt, step, ids, adv, frames,
    w_x, w_bc, every, out_bc, cross_bc, dt_all, acc, back, halves, mine, tile, tiles_t, tiles_p, picked, given,
    x_s, x_r, z_s, z_r, d_s, d_r, r_s, r_r, h_s, h_r, p_s, p_r, q_s, q_r, g_s, g_r, c_s, c_r, w_sem,
):
    parts = 2 * shards
    g, s, t = place()
    me = g * shards + s
    width = acc.shape[-1]
    sub = merged.shape[1]
    per = merged.shape[-1] // width
    count = shards * tensors * sub
    nq = grads.shape[0]
    span = shards // nq
    deep = tensors * sub

    def peer(i):
        p = lax.rem(me + i, parts)
        return p, (p // shards, lax.rem(p, shards), t)

    loads = [
        pltpu.make_async_copy(src, dst, w_sem.at[n])
        for n, (src, dst) in enumerate(((w_x_hbm, w_x), (w_bc_hbm, w_bc)))
    ]
    for load in loads:
        load.start()
    wide = w_x.shape[1] // shards
    pairs = shards // (w_bc.shape[1] // (2 * STATE))
    greet(parts, shards, tensors, per)

    def send_dt(i):
        p, device = peer(i)
        return rcopy(gdt, dt_all.at[me], d_s.at[i], d_r.at[i], device)

    def cross(j, q):
        at = every.at[g, j, q, :, :wide]
        return rcopy(at, at, x_s.at[j, q], x_r.at[j, q], (1 - g, s, t))

    def bc_cross(j, q):
        n = j // pairs
        return rcopy(out_bc.at[n, q], cross_bc.at[n, q], c_s.at[n, q], c_r.at[n, q], (1 - g, s, t))

    def right(j, q):
        return rcopy(every.at[g, j, q], every.at[g, j, q], z_s.at[0, j, q], z_r.at[j, q], (g, s + 1, t))

    def left(j, q):
        return rcopy(every.at[g, j, q], every.at[g, j, q], z_s.at[1, j, q], z_r.at[j, q], (g, s - 1, t))

    def each_way(j, q, what):
        @pl.when((j <= s) & (s < shards - 1))
        def _():
            what(right(j, q))

        @pl.when((j >= s) & (s > 0))
        def _():
            what(left(j, q))

        what(cross(j, q))

    for q in range(nq):
        every[g, s, q] = grads[q]
        each_way(s, q, lambda c: c.start())
    for i in range(1, parts):
        send_dt(i).start()
    dt_all[me] = gdt[...]
    for i in range(1, parts):
        q = lax.rem(me + parts - i, parts)
        p, device = peer(i)
        rcopy(gdt, dt_all.at[q], d_s.at[i], d_r.at[i], device).wait_recv()
    for gg in range(2):
        stack = jnp.concatenate([dt_all[gg * shards + k] for k in range(shards)], axis=0)
        acc[gg] = jnp.dot(
            stack.T.astype(BF16), wdt[...], preferred_element_type=F32
        ).reshape(nq, count // nq, width)

    nt = (((1,), (1,)), ((), ()))

    def add(gg, j, q):
        acc[gg, q] += lax.dot_general(
            every[gg, j, q, :, :wide], columns_of(w_x, j, wide), nt, preferred_element_type=F32
        )

    def add_bc(gg, j, q, ref):
        n = j // pairs
        acc[gg, q] += lax.dot_general(
            ref[n, q], columns_of(w_bc, n, 2 * STATE), nt, preferred_element_type=F32
        )

    def near(i):
        return far_first(shards - 1 - i, s, shards)

    def add_cross(i, q):
        j = near(i)
        at = every.at[1 - g, j, q, :, :wide]
        rcopy(at, at, x_s.at[j, q], x_r.at[j, q], (1 - g, s, t)).wait_recv()
        add(1 - g, j, q)
        if i % pairs == pairs - 1:
            bc_cross(j, q).wait_recv()
            add_bc(1 - g, j, q, cross_bc)

    for load in loads:
        load.wait()
    for q in range(nq):
        add(g, s, q)
    for i in range(1, shards):
        j = near(i)
        for q in range(nq):
            rcopy(
                every.at[g, j, q], every.at[g, j, q], x_s.at[j, q], z_r.at[j, q], (1 - g, s, t)
            ).wait_recv()
            each_way(j, q, lambda c: c.start())
            if i % pairs == pairs - 1:
                both = every[g, j, q, :, wide:].astype(F32)
                for n in range(1, pairs):
                    both = both + every[g, near(i - n), q, :, wide:].astype(F32)
                out_bc[j // pairs, q] = both.astype(BF16)
                bc_cross(j, q).start()
                add_bc(g, j, q, out_bc)
            add(g, j, q)
            add_cross(i - 1, q)

    steps = bits(tensors)

    def reduce_tensor(gg):
        for c in range(shards):
            q, k = c // span, c % span
            back[gg, c] = (
                acc[gg, q, k * deep : (k + 1) * deep].astype(BF16).reshape(tensors, sub, width)
            )
        low, size = 0, tensors
        for n, m in enumerate(steps):
            size //= 2
            bit = lax.rem(t // m, 2)
            keep, give = low + bit * size, low + (1 - bit) * size
            at = tensors - 2 * size
            copy = rcopy(
                back.at[gg, :, pl.ds(give, size)], halves.at[gg, :, pl.ds(at, size)],
                r_s.at[gg, n], r_r.at[gg, n], (g, s, t ^ m),
            )
            copy.start()
            copy.wait_recv()
            back[gg, :, pl.ds(keep, size)] = (
                back[gg, :, pl.ds(keep, size)].astype(F32)
                + halves[gg, :, at : at + size].astype(F32)
            ).astype(BF16)
            copy.wait_send()
            low = keep
        return low

    def spot_of(tt):
        low, size = 0, tensors
        for m in steps:
            size //= 2
            low = low + lax.rem(tt // m, 2) * size
        return low

    holder = me // per
    slot = lax.rem(me, per)

    def send_home(gg, k):
        return rcopy(
            back.at[gg, k, spot], mine.at[spot, slot], h_s.at[gg * shards + k], h_r.at[spot, slot],
            (gg, k, holder),
        )

    def home_all(gg, what):
        for k in range(shards):
            @pl.when((gg * shards + k != me) | (holder != t))
            def _():
                what(send_home(gg, k))

    def send_tile(gg, k):
        return rcopy(
            tile.at[gg], tiles_p.at[me], q_s.at[gg * shards + k], q_r.at[me], (gg, k, t)
        )

    def squares(gg):
        total = jnp.zeros((8, 128), F32)
        for k in range(shards):
            sq = back[gg, k, spot].astype(F32)
            sq = jnp.sum((sq * sq).reshape(sub // 8, 8, width), axis=0)
            for b in range(width // 128):
                total = total + sq[:, b * 128 : (b + 1) * 128]
        tile[gg] = total

    spot = reduce_tensor(g)
    squares(g)
    for k in range(shards):
        @pl.when(k != s)
        def _():
            send_tile(g, k).start()

    home_all(g, lambda c: c.start())
    tiles_p[me] = tile[g]

    @pl.when(holder == t)
    def _():
        mine[spot, slot] = back[g, s, spot]

    for q in range(nq):
        add_cross(shards - 1, q)
    spot = reduce_tensor(1 - g)
    squares(1 - g)
    for k in range(shards):
        send_tile(1 - g, k).start()
    home_all(1 - g, lambda c: c.start())
    for i in range(1, parts):
        p, device = peer(i)
        rcopy(tiles_p.at[p], tiles_p.at[p], q_s.at[p], q_r.at[p], device).wait_recv()
    total = tiles_p[0]
    for p in range(1, parts):
        total = total + tiles_p[p]
    tile[2] = total

    def share_t(m):
        return rcopy(tile.at[2], tiles_t.at[m], p_s.at[m], p_r.at[m], (g, s, t ^ m))

    for m in range(1, tensors):
        share_t(m).start()
    for h in range(per):
        for m in range(tensors):
            at = spot_of(t ^ m)

            @pl.when((t * per + h != me) | (m != 0))
            def _():
                rcopy(
                    mine.at[at, h], mine.at[at, h], h_s.at[0], h_r.at[at, h], (1 - g, s, t)
                ).wait_recv()

    for m in range(1, tensors):
        share_t(m).wait_recv()
        total = total + tiles_t[m]
    entries = count * parts * width
    scale = lax.rsqrt(jnp.sum(total, keepdims=True) / entries + 1e-06)
    for n in range(tensors):
        move = step[n] * scale
        for h in range(per):
            at = slice(h * width, (h + 1) * width)
            adv[n, :, at] = (
                merged[n, :, at].astype(F32) + move * mine[n, h].astype(F32)
            ).astype(BF16)

    slots = picked.shape[1]
    hot = one_hot(ids[0, 0:1], s, deep).T[: shards * slots].astype(BF16)
    chosen = jnp.dot(hot, adv[...].reshape(deep, -1), preferred_element_type=F32)
    picked[...] = chosen.astype(BF16).reshape(picked.shape)

    def give_back(i):
        k = lax.rem(s + i, shards)
        return rcopy(picked.at[k], given.at[i], g_s.at[i], g_r.at[i], (g, k, t))

    for i in range(1, shards):
        give_back(i).start()
    total = picked[s].astype(F32)
    for i in range(1, shards):
        give_back(i).wait_recv()
        total = total + given[i].astype(F32)
    frames[...] = total[: frames.shape[0]].astype(BF16)

    for i in range(1, parts):
        send_dt(i).wait_send()
    for m in range(1, tensors):
        share_t(m).wait_send()
    for i in range(1, shards):
        give_back(i).wait_send()
    home_all(g, lambda c: c.wait_send())
    home_all(1 - g, lambda c: c.wait_send())
    for k in range(shards):
        @pl.when(k != s)
        def _():
            send_tile(g, k).wait_send()

        send_tile(1 - g, k).wait_send()

    def end(j, carry):
        for q in range(nq):
            @pl.when(lax.rem(j, pairs) == 0)
            def _():
                bc_cross(j, q).wait_send()

            each_way(j, q, lambda c: c.wait_send())
        return carry

    lax.fori_loop(0, shards, end, 0)


def backward(merged, grads, gdt, w_x, w_bc, wdt, direction, ids, slots, frames, shards):
    parts = 2 * shards
    tensors, sub, held = merged.shape
    rows = tensors * sub
    width = w_x.shape[0]
    cols = grads.shape[1]
    count = rows * shards
    per = held // width
    heads = gdt.shape[0]
    nq = 2
    maps = w_bc.shape[1] // (2 * STATE)
    block = (count // nq, cols)
    dma = pltpu.SemaphoreType.DMA
    levels = len(bits(tensors))
    adv, returned = pl.pallas_call(
        functools.partial(backward_kernel, shards, tensors),
        out_shape=(
            jax.ShapeDtypeStruct((tensors, sub, held), BF16),
            jax.ShapeDtypeStruct((frames, held), BF16),
        ),
        in_specs=[
            pl.BlockSpec(memory_space=pl.ANY if n in (3, 4) else pltpu.VMEM) for n in range(8)
        ],
        out_specs=[pl.BlockSpec(memory_space=pltpu.VMEM)] * 2,
        scratch_shapes=[
            pltpu.VMEM(w_x.shape, BF16),
            pltpu.VMEM(w_bc.shape, BF16),
            pltpu.VMEM((2, shards, nq) + block, BF16),
            pltpu.VMEM((maps, nq, count // nq, 2 * STATE), BF16),
            pltpu.VMEM((maps, nq, count // nq, 2 * STATE), BF16),
            pltpu.VMEM((parts, heads, count), F32),
            pltpu.VMEM((2, nq, count // nq, width), F32),
            pltpu.VMEM((2, shards, tensors, sub, width), BF16),
            pltpu.VMEM((2, shards, tensors, sub, width), BF16),
            pltpu.VMEM((tensors, per, sub, width), BF16),
            pltpu.VMEM((3, 8, 128), F32),
            pltpu.VMEM((tensors, 8, 128), F32),
            pltpu.VMEM((parts, 8, 128), F32),
            pltpu.VMEM((shards, slots, held), BF16),
            pltpu.VMEM((shards, slots, held), BF16),
            dma((shards, nq)), dma((shards, nq)),
            dma((2, shards, nq)), dma((shards, nq)),
            dma((parts,)), dma((parts,)),
            dma((2, levels)), dma((2, levels)),
            dma((parts,)), dma((tensors, per)),
            dma((tensors,)), dma((tensors,)),
            dma((parts,)), dma((parts,)),
            dma((shards,)), dma((shards,)),
            dma((maps, nq)), dma((maps, nq)),
            dma((2,)),
        ],
        compiler_params=pltpu.CompilerParams(
            collective_id=1, has_side_effects=True, vmem_limit_bytes=VMEM_BYTES
        ),
        name="gather_project_step",
    )(
        merged,
        grads.reshape((nq,) + block),
        gdt,
        w_x,
        w_bc,
        wdt,
        direction.reshape(tensors, sub, 1),
        ids,
    )
    return adv.reshape(rows, held), returned


def in_vmem(groups, shards, tensors, rows, width, cols, slots, pairs):
    if groups != 2 or shards % 2 or tensors & (tensors - 1) or rows % (16 * tensors):
        return False
    if rows != 128 or slots * shards > 128 or shards != 4 or pairs not in (1, 2):
        return False
    if width % 128 or cols % 128 or shards * width * 2 % tensors:
        return False
    count = rows * shards
    lines = 2 * count * cols * (4 * shards + 1)
    sums = 2 * count * width * 4 + 4 * count * cols * shards
    return max(lines, sums) + 2 * width * cols * shards + 8 * count * width < VMEM_BYTES // 2


def mixer_grad(x, b, c, pdt, probe, seg, dt_bias, decay_rate, skip_gain):
    count, heads = pdt.shape
    shifted = pdt + dt_bias[None, :]
    dt = jax.nn.softplus(shifted).T
    ld = jnp.cumsum(-dt * decay_rate[:, None], axis=1)
    position = jnp.arange(count)
    visible = (seg[:, None] == seg[None, :]) & (position[:, None] >= position[None, :])
    gap = ld[:, :, None] - ld[:, None, :]
    decay = jnp.where(visible[None], jnp.exp(jnp.where(visible[None], gap, 0.0)), 0.0)
    xh = x.astype(BF16).reshape(count, heads, HEAD_DIM)
    ph = probe.reshape(count, heads, HEAD_DIM)
    bb, cb = b.astype(BF16), c.astype(BF16)
    scores = jnp.dot(cb, bb.T, preferred_element_type=F32)
    pairs = jnp.einsum("thp,shp->hts", ph, xh, preferred_element_type=F32)
    mixed = decay * scores[None]
    grad_x = jnp.einsum("hts,thp->shp", mixed.astype(BF16), ph, preferred_element_type=F32)
    grad_x = grad_x * dt.T[:, :, None] + skip_gain[None, :, None] * ph.astype(F32)
    weighted = mixed * pairs
    col = jnp.sum(weighted, axis=1)
    row = jnp.sum(weighted * dt[:, None, :], axis=2)
    grad_s = jnp.sum(decay * pairs * dt[:, None, :], axis=0).astype(BF16)
    grad_c = jnp.dot(grad_s, bb, preferred_element_type=F32)
    grad_b = jnp.dot(grad_s.T, cb, preferred_element_type=F32)
    grad_ld = row - col * dt
    later = jnp.cumsum(grad_ld[:, ::-1], axis=1)[:, ::-1]
    grad_dt = (col - decay_rate[:, None] * later).T * jax.nn.sigmoid(shifted)
    return grad_x.reshape(count, -1), grad_b, grad_c, grad_dt


def by_collectives(
    tokens,
    frame_feats,
    w_proj,
    frame_pos,
    segments,
    signs,
    w_x,
    w_bc,
    w_dt,
    dt_bias,
    decay_rate,
    skip_gain,
    probe,
):
    rows = tokens.shape[1]
    groups, shards, tensors = (lax.axis_size(a) for a in ("group", "seq", "tensor"))
    g, s, t = (lax.axis_index(a) for a in ("group", "seq", "tensor"))
    parts = groups * shards
    count = rows * shards
    width = w_x.shape[0]
    heads = w_dt.shape[1] // shards
    per_group = w_dt.shape[1] * 2 * STATE // w_bc.shape[1]
    cols_x = heads * HEAD_DIM
    group_of = [(k * heads) // per_group for k in range(shards)]
    cols = cols_x + 2 * STATE + heads

    feats, pos = (
        lax.all_to_all(frame_feats[0], "seq", split_axis=0, concat_axis=0, tiled=True),
        lax.all_to_all(frame_pos[0], "seq", split_axis=0, concat_axis=0, tiled=True),
    )
    local_pos = pos - s * rows
    arrived = jnp.dot(feats, w_proj, preferred_element_type=F32).astype(BF16)
    merged = tokens[0].at[local_pos].set(arrived)

    sub = rows // tensors
    f = lax.all_to_all(merged, "tensor", split_axis=0, concat_axis=1, tiled=True)
    f = f.reshape(sub, parts, width).transpose(1, 0, 2)
    f = lax.all_to_all(f, ("group", "seq"), split_axis=0, concat_axis=0, tiled=True)
    f = lax.all_gather(f, "tensor", axis=1, tiled=True)
    f = f.reshape(groups, count, width)

    weights = jnp.stack(
        [
            jnp.concatenate(
                [
                    w_x[:, k * cols_x : (k + 1) * cols_x],
                    w_bc[:, group_of[k] * 2 * STATE : (group_of[k] + 1) * 2 * STATE],
                    w_dt[:, k * heads : (k + 1) * heads],
                ],
                axis=1,
            )
            for k in range(shards)
        ]
    )
    partial = jnp.einsum("gtk,skc->gstc", f, weights, preferred_element_type=F32).astype(BF16)
    proj = lax.psum_scatter(
        partial.reshape(parts, count, cols), ("group", "seq"), scatter_dimension=0, tiled=False
    ).astype(F32)

    seg = lax.all_gather(segments[0], "seq", axis=0, tiled=True)
    prb = lax.all_to_all(
        probe[0].reshape(rows, shards, cols_x).transpose(1, 0, 2),
        "seq",
        split_axis=0,
        concat_axis=0,
        tiled=True,
    ).reshape(count, cols_x)

    def own(v):
        return lax.dynamic_slice(v, (s * heads,), (heads,))

    grads = mixer_grad(
        proj[:, :cols_x],
        proj[:, cols_x : cols_x + STATE],
        proj[:, cols_x + STATE : cols_x + 2 * STATE],
        proj[:, cols_x + 2 * STATE :],
        prb,
        seg,
        own(dt_bias),
        own(decay_rate),
        own(skip_gain),
    )
    grads = jnp.concatenate([v.astype(BF16) for v in grads], axis=1)
    every = lax.all_gather(grads, ("group", "seq"), axis=0, tiled=False)
    every = every.reshape(groups, shards, count, cols)
    back = jnp.einsum("gstc,skc->gtk", every, weights, preferred_element_type=F32).astype(BF16)

    back = back.reshape(parts, tensors, sub, width).transpose(1, 0, 2, 3)
    back = lax.all_to_all(back, "tensor", split_axis=0, concat_axis=0, tiled=True)
    summed = jnp.sum(back.astype(F32), axis=0)
    squares = jnp.sum(summed.reshape(groups, -1) ** 2, axis=1)
    squares = lax.psum(squares, ("group", "seq", "tensor"))[g]
    home = lax.all_to_all(
        summed.astype(BF16), ("group", "seq"), split_axis=0, concat_axis=0, tiled=True
    )
    home = home.transpose(1, 0, 2).reshape(sub, tensors, -1).transpose(1, 0, 2)
    gradient = lax.all_to_all(home, "tensor", split_axis=0, concat_axis=0, tiled=True)
    gradient = gradient.reshape(rows, -1).astype(F32)

    entries = count * parts * width
    grad_scale = jnp.sqrt(squares / entries + 1e-06)
    direction = (2 * signs[0] - 1).astype(F32)[:, None]
    adv = (merged.astype(F32) + 0.5 * direction * gradient / grad_scale).astype(BF16)
    picked = adv[local_pos]
    returned = lax.all_to_all(picked, "seq", split_axis=0, concat_axis=0, tiled=True)
    return (adv[None], returned[None])


def body(*arrays):
    tokens, frame_feats, w_x, w_dt = arrays[0], arrays[1], arrays[6], arrays[8]
    sizes = tuple(lax.axis_size(a) for a in ("group", "seq", "tensor"))
    cols = w_dt.shape[1] // sizes[1] * HEAD_DIM + 2 * STATE
    slots = -(-frame_feats.shape[1] // 16) * 16
    pairs = sizes[1] * 2 * STATE // arrays[7].shape[1]
    if in_vmem(*sizes, tokens.shape[1], w_x.shape[0], cols, slots, pairs):
        return by_kernels(slots, *arrays)
    return by_collectives(*arrays)


def by_kernels(
    slots,
    tokens,
    frame_feats,
    w_proj,
    frame_pos,
    segments,
    signs,
    w_x,
    w_bc,
    w_dt,
    dt_bias,
    decay_rate,
    skip_gain,
    probe,
):
    shards, tensors = lax.axis_size("seq"), lax.axis_size("tensor")
    s = lax.axis_index("seq")
    frames = frame_feats.shape[1]
    heads = w_dt.shape[1] // shards
    ffeat = jnp.pad(frame_feats[0], ((0, slots - frames), (0, 0)))
    lane = jnp.full((shards, slots), -1, jnp.int32)
    lane = lax.dynamic_update_slice(lane, frame_pos, (s, 0)).reshape(1, -1)
    lane = jnp.pad(lane, ((0, 0), (0, 128 - shards * slots)), constant_values=-1)
    ids = jnp.concatenate([jnp.broadcast_to(v, (8, 128)) for v in (lane, segments)], axis=0)
    w_step = w_dt.T
    merged, proj, raw, prb, ids = forward(
        tokens[0], ffeat, ids, w_proj, probe[0], w_x, w_bc, w_step, shards, tensors, heads
    )
    params = jnp.stack([dt_bias, decay_rate, skip_gain], axis=1)
    params = lax.dynamic_slice(params, (s * heads, 0), (heads, 3))
    grads, gdt = mixer(proj, raw, prb, ids, params)
    direction = 0.5 * (2 * signs[0] - 1).astype(F32)
    adv, returned = backward(
        merged, grads, gdt, w_x, w_bc, w_step, direction, ids, slots, frames, shards
    )
    return (adv[None], returned[None])


def solution(mesh):
    return jax.shard_map(
        body,
        mesh=mesh,
        in_specs=(
            P("group", "seq", "tensor"),
            P("group", "seq", None),
            P(None, "tensor"),
            P("group", "seq"),
            P("group", "seq"),
            P("group", "seq"),
            P(("group", "seq"), "tensor"),
            P(("group", "seq"), "tensor"),
            P(("group", "seq"), "tensor"),
            P("tensor"),
            P("tensor"),
            P("tensor"),
            P("group", "seq", "tensor"),
        ),
        out_specs=(P("group", "seq", "tensor"), P("group", "seq", "tensor")),
        check_vma=False,
    )
```
